128 devices in a mesh: shard: 16 (over z, y), ctx: 2 (over x_lo), tp: 4 (over x_hi, core).
Axes of the slice: x: 4 (x_hi: 2, x_lo: 2; x = x_hi * 2 + x_lo), y: 4, z: 4, core: 2. Of those that a mesh axis runs over, the one named last changes fastest.
Arguments:
- tokens: bfloat16 [16, 1024, 1088], P('shard', ('ctx', 'tp')), may hold values from -6 to 6
- cotangent: bfloat16 [16, 1024, 1088], P('shard', ('ctx', 'tp')), may hold values from -6 to 6
- block_order: int32 [4], replicated, may hold values from 0 to 3, each once
- head_count: int32 [4], replicated, may hold values from 3 to 5, as said below
- ln_gain: float32 [2, 2, 1088], replicated, may hold values from 0.1 to 1.9
- ln_bias: float32 [2, 2, 1088], replicated, may hold values from -1.5 to 1.5
- w_qkv: bfloat16 [2, 4, 5, 1088, 192], P(None, 'tp', None, ('shard', 'ctx')), may hold values from -0.1875 to 0.1875
- b_qv: float32 [2, 4, 5, 128], P(None, 'tp'), may hold values from -3 to 3
- w_out: bfloat16 [2, 4, 5, 64, 1088], P(None, 'tp', None, None, ('shard', 'ctx')), may hold values from -0.75 to 0.75
- b_out: float32 [2, 1088], replicated, may hold values from -3 to 3
- w_fc: bfloat16 [2, 1088, 4352], P(None, ('shard', 'ctx'), 'tp'), may hold values from -0.1875 to 0.1875
- b_fc: float32 [2, 4352], P(None, 'tp'), may hold values from -3 to 3
- w_down: bfloat16 [2, 4352, 1088], P(None, 'tp', ('shard', 'ctx')), may hold values from -0.09375 to 0.09375
- b_down: float32 [2, 1088], replicated, may hold values from -3 to 3
Outputs:
- mixed: bfloat16 [16, 1024, 1088], P('shard', ('ctx', 'tp'))
- grad_tokens: float32 [16, 1024, 1088], P('shard', ('ctx', 'tp'))
- grad_ln_gain: float32 [2, 2, 1088], replicated
- grad_ln_bias: float32 [2, 2, 1088], replicated
- grad_w_qkv: float32 [2, 4, 5, 1088, 192], P(None, 'tp', None, ('shard', 'ctx'))
- grad_b_qv: float32 [2, 4, 5, 128], P(None, 'tp')
- grad_w_out: float32 [2, 4, 5, 64, 1088], P(None, 'tp', None, None, ('shard', 'ctx'))
- grad_b_out: float32 [2, 1088], replicated
- grad_w_fc: float32 [2, 1088, 4352], P(None, ('shard', 'ctx'), 'tp')
- grad_b_fc: float32 [2, 4352], P(None, 'tp')
- grad_w_down: float32 [2, 4352, 1088], P(None, 'tp', ('shard', 'ctx'))
- grad_b_down: float32 [2, 1088], replicated
The draws below stay inside these ranges and needn't reach their ends.
Inputs may be any that keep to these rules, and one draw needn't show every extreme that they name: Each stored block of 256 rows of a sequence holds the positions of block block_order[b]; each block number appears once. `head_count`: the counts sum to 17; at least one rank, drawn from the seed, uses all 5 slots; no rank uses fewer than 3; a rank uses its slots from the first.
All inputs are finite; a program needn't handle non-finite values.
Results may differ from the reference program's by a relative error of at most 0.025.
Values may be sent and summed in bfloat16 or wider, within the bound.
No kernel may reach another device: no remote copies, remote signals or barrier semaphores. Data moves between devices by JAX's collectives and lax.ppermute only.
A program may use at most 192 MiB of HBM per device.

```python
import jax
import jax.numpy as jnp
from jax import lax

D = 1088
HEADS = 17
HD = 64
FF = 4352
LEN = 1024
LAYERS = 2
SLOTS = 5
SEQS = 16
N_CTX = 2
N_TP = 4


def draw_head_count(key, part):
    key = jax.random.fold_in(key, 7)
    full_rank = jax.random.randint(jax.random.fold_in(key, 1), (), 0, N_TP).astype(jnp.int32)
    moved = jax.random.randint(jax.random.fold_in(key, 2), (), 0, 2).astype(jnp.int32)
    extra = HEADS % N_TP
    allowed = 1 if extra + 2 <= N_TP else 0
    moved = moved * allowed
    offset = (jnp.arange(N_TP, dtype=jnp.int32) - full_rank + N_TP) % N_TP
    counts = HEADS // N_TP + (offset < extra).astype(jnp.int32)
    counts = counts + moved * (offset == extra).astype(jnp.int32) - moved * (offset == extra + 1).astype(jnp.int32)
    return counts.astype(jnp.int32)


def block_levels(own_key, shape, cuts, smallest, top_value):
    level = 1.0
    for dim, shards_of in cuts:
        steps = jax.random.uniform(jax.random.fold_in(jax.random.fold_in(own_key, 6), dim), (shards_of,), jnp.float32, smallest / len(cuts), top_value / len(cuts))
        level = level * jnp.repeat(jnp.exp(steps), shape[dim] // shards_of).reshape((-1,) + (1,) * (len(shape) - 1 - dim))
    return level


def scatter_about(own_key, shape, deviation, bound, cuts=(), kind=jnp.bfloat16):
    array = deviation * jax.random.normal(own_key, shape, jnp.float32)
    if cuts:
        array = array * block_levels(own_key, shape, cuts, -0.22, 0.18)
    return jnp.clip(array, -bound, bound).astype(kind)


def setup_inputs(seed: int = 0) -> dict:
    streams_of = jax.random.split(jax.random.key(seed), 15)
    tokens = scatter_about(streams_of[0], (SEQS, LEN, D), 1.0, 6.0, ((0, 16), (1, 8)))
    cotangent = scatter_about(streams_of[1], (SEQS, LEN, D), 1.0, 6.0, ((0, 16), (1, 8)))
    block_order = jax.random.permutation(streams_of[2], 2 * N_CTX).astype(jnp.int32)
    head_count = draw_head_count(jax.random.fold_in(streams_of[14], 71), 0)
    ln_gain = jnp.clip(1.0 + 0.18 * jax.random.normal(streams_of[4], (LAYERS, 2, D), jnp.float32), 0.1, 1.9)
    ln_bias = scatter_about(streams_of[5], (LAYERS, 2, D), 0.3, 1.5, (), jnp.float32)
    w_qkv = scatter_about(streams_of[6], (LAYERS, N_TP, SLOTS, D, 3 * HD), D ** -0.5, 0.1875, ((1, 4), (3, 32)))
    b_qv = scatter_about(streams_of[7], (LAYERS, N_TP, SLOTS, 2 * HD), 0.5, 3.0, ((1, 4),), jnp.float32)
    w_out = scatter_about(streams_of[8], (LAYERS, N_TP, SLOTS, HD, D), (LEN // 16) ** -0.5, 0.75, ((1, 4), (4, 32)))
    b_out = scatter_about(streams_of[9], (LAYERS, D), 0.5, 3.0, (), jnp.float32)
    w_fc = scatter_about(streams_of[10], (LAYERS, D, FF), D ** -0.5, 0.1875, ((1, 32), (2, 4)))
    b_fc = scatter_about(streams_of[11], (LAYERS, FF), 0.5, 3.0, ((1, 4),), jnp.float32)
    w_down = scatter_about(streams_of[12], (LAYERS, FF, D), FF ** -0.5, 0.09375, ((1, 4), (2, 32)))
    b_down = scatter_about(streams_of[13], (LAYERS, D), 0.5, 3.0, (), jnp.float32)
    return {"tokens": tokens, "cotangent": cotangent, "block_order": block_order, "head_count": head_count, "ln_gain": ln_gain, "ln_bias": ln_bias, "w_qkv": w_qkv, "b_qv": b_qv, "w_out": w_out, "b_out": b_out, "w_fc": w_fc, "b_fc": b_fc, "w_down": w_down, "b_down": b_down}


@jax.custom_vjp
def low(v):
    return lax.optimization_barrier(v.astype(jnp.bfloat16)).astype(jnp.float32)

@jax.custom_vjp
def low_back(v):
    return v

def low_keep(v):
    return (low(v), None)

def low_pass(kept, grad):
    return (grad,)

def back_keep(v):
    return (v, None)

def back_low(kept, grad):
    return (low(grad),)
low.defvjp(low_keep, low_pass)
low_back.defvjp(back_keep, back_low)
EPS = 1e-05
HIGHEST = lax.Precision.HIGHEST

def layer_norm(values_in, gain, shift):
    average = lax.optimization_barrier(jnp.mean(values_in, axis=-1, keepdims=True))
    centred = values_in - average
    variance = lax.optimization_barrier(jnp.mean(centred * centred, axis=-1, keepdims=True))
    return centred * lax.rsqrt(variance + EPS) * gain + shift

def place_rows(block_order):
    parts_count = block_order.shape[0]
    block_rows = LEN // parts_count
    row_index = jnp.arange(LEN, dtype=jnp.int32)
    onehot = row_index[:, None] // block_rows == jnp.arange(parts_count, dtype=jnp.int32)[None, :]
    chosen = lax.optimization_barrier(jnp.sum(jnp.where(onehot, block_order[None, :], 0), axis=1)).astype(jnp.int32)
    return chosen * block_rows + row_index % block_rows

def attend(queries, keys_all, values_all, places):
    query_rows = min(LEN, 512)
    blocks = LEN // query_rows
    split_queries = jnp.moveaxis(queries.reshape(N_TP, SLOTS, blocks, query_rows, HD), 2, 0)
    split_places = places.reshape(blocks, query_rows)
    score_scale = HD ** (-0.5)

    @jax.checkpoint
    def one_block(pieces):
        block_queries, block_places = pieces
        raw_scores = jnp.einsum('rhqe,rhke->rhqk', block_queries, keys_all, precision=HIGHEST) * score_scale
        scores = low_back(raw_scores)
        allowed = places[None, :] <= block_places[:, None]
        masked = jnp.where(allowed, scores, -1e+30)
        highest = lax.optimization_barrier(jnp.max(masked, axis=-1, keepdims=True))
        exponent = jnp.exp(masked - highest)
        attn_probs = low(exponent / lax.optimization_barrier(jnp.sum(exponent, axis=-1, keepdims=True)))
        return jnp.einsum('rhqk,rhke->rhqe', attn_probs, values_all, precision=HIGHEST)
    result = lax.map(one_block, (split_queries, split_places))
    return jnp.moveaxis(result, 0, 2).reshape(N_TP, SLOTS, LEN, HD)

def layer(hidden_in, places, slot_live, params):
    gains, shifts, weight_qkv, head_bias, weight_out, bias_out, weight_fc, bias_fc, weight_down, bias_down = params
    normed = low(layer_norm(hidden_in, gains[0], shifts[0]))
    projected = jnp.einsum('td,rhde->rhte', normed, weight_qkv, precision=HIGHEST)
    queries = low(low_back(projected[..., :HD] + head_bias[:, :, None, :HD]))
    keys_all = low(low_back(projected[..., HD:2 * HD]))
    values_all = low(low_back(projected[..., 2 * HD:] + head_bias[:, :, None, HD:]))
    attended = attend(queries, keys_all, values_all, places) * slot_live[:, :, None, None]
    attended = low(low_back(attended))
    branch = low_back(jnp.einsum('rhte,rhed->td', attended, weight_out, precision=HIGHEST) + bias_out)
    middle = hidden_in + branch
    normed_two = low(layer_norm(middle, gains[1], shifts[1]))
    inner_pre = low_back(jnp.dot(normed_two, weight_fc, precision=HIGHEST) + bias_fc)
    activated = low(jax.nn.gelu(inner_pre, approximate=False))
    branch_two = low_back(jnp.dot(activated, weight_down, precision=HIGHEST) + bias_down)
    return middle + branch_two

def reference(tokens, cotangent, block_order, head_count, ln_gain, ln_bias, w_qkv, b_qv, w_out, b_out, w_fc, b_fc, w_down, b_down):
    places = place_rows(block_order)
    slot_live = (jnp.arange(SLOTS, dtype=jnp.int32)[None, :] < head_count[:, None]).astype(jnp.float32)
    params = (ln_gain, ln_bias, w_qkv.astype(jnp.float32), b_qv, w_out.astype(jnp.float32), b_out, w_fc.astype(jnp.float32), b_fc, w_down.astype(jnp.float32), b_down)

    def forward(sequence_in, weights):
        hidden = sequence_in
        for layer_idx in range(LAYERS):
            hidden = layer(hidden, places, slot_live, tuple((item[layer_idx] for item in weights)))
        return hidden

    def per_sequence(totals, inputs):
        sequence_in, sequence_cot = inputs
        result, pullback = jax.vjp(forward, sequence_in.astype(jnp.float32), params)
        grad_in, grad_params = pullback(sequence_cot.astype(jnp.float32))
        totals = jax.tree.map(jnp.add, totals, grad_params)
        return (totals, (result.astype(jnp.bfloat16), grad_in))
    zero_grads = jax.tree.map(jnp.zeros_like, params)
    totals, (outputs, grad_tokens) = lax.scan(per_sequence, zero_grads, (tokens, cotangent))
    return (outputs, grad_tokens) + tuple(totals)
```

```python
import jax
import jax.numpy as jnp
from jax import lax
from jax.sharding import PartitionSpec as P

D = 1088
HD = 64
LAYERS = 2
EPS = 1e-05
SHARDS = 16
CHUNK = 34
WIDE = 36
DP = 2 * SHARDS * WIDE
HEADS_HERE = 3
QW = HEADS_HERE * HD
FH = 544
FP = 640
ROWS = 128
BF = jnp.bfloat16
F32 = jnp.float32
LINE = ("ctx", "tp")


def line_perm(target):
    pairs = []
    for c in range(2):
        for h in range(2):
            for k in range(2):
                x2, k2 = target(2 * h + c, k)
                pairs.append((c * 4 + h * 2 + k, (x2 % 2) * 4 + (x2 // 2) * 2 + k2))
    return pairs


def swap_core(v):
    return lax.ppermute(v, LINE, line_perm(lambda x, k: (x, 1 - k)))


def swap_x(v, m):
    return lax.ppermute(v, LINE, line_perm(lambda x, k: (x ^ m, k)))


def swap_ctx(v):
    return lax.ppermute(v, "ctx", [(0, 1), (1, 0)])


def swap_shard(v, m):
    return lax.ppermute(v, "shard", [(i, i ^ m) for i in range(SHARDS)])


def gather_rows(piece):
    mine = jnp.concatenate([piece] + [swap_x(piece, m) for m in (1, 2, 3)], axis=0)
    return jnp.concatenate([mine, swap_core(mine)], axis=0)


def sum_rows(partial):
    half = 4 * ROWS
    arrived = swap_core(partial[half:].astype(BF))
    chip = partial[:half] + arrived.astype(F32)
    low = chip.astype(BF)
    parts = [swap_x(low[m * ROWS : (m + 1) * ROWS], m).astype(F32) for m in (1, 2, 3)]
    return (chip[:ROWS] + parts[0]) + (parts[1] + parts[2])


def sum_shards(v):
    v = (v + swap_shard(v, 1)) + (swap_shard(v, 2) + swap_shard(v, 3))
    return (v + swap_shard(v, 4)) + (swap_shard(v, 8) + swap_shard(v, 12))


def sum_line(v):
    v = v + swap_core(v)
    return (v + swap_x(v, 1)) + (swap_x(v, 2) + swap_x(v, 3))


def dot(a, b, dims):
    return lax.dot_general(a, b, (dims, ((), ())), preferred_element_type=F32)


def norm_forward(x, gain, shift, mask):
    mean = jnp.sum(x, axis=-1, keepdims=True) * (1.0 / D)
    centred = (x - mean) * mask
    var = jnp.sum(centred * centred, axis=-1, keepdims=True) * (1.0 / D)
    rstd = lax.rsqrt(var + EPS)
    xhat = centred * rstd
    return (xhat * gain + shift).astype(BF), xhat, rstd


def norm_backward(dy, xhat, rstd, gain, mask):
    e = dy * gain
    mean_e = jnp.sum(e, axis=-1, keepdims=True) * (1.0 / D)
    mean_ex = jnp.sum(e * xhat, axis=-1, keepdims=True) * (1.0 / D)
    dx = rstd * (e - mean_e - xhat * mean_ex) * mask
    return dx, jnp.sum(dy * xhat, axis=0), jnp.sum(dy, axis=0)


def gelu_exact(v):
    return jax.nn.gelu(v, approximate=False)


def split_heads(v):
    return jnp.moveaxis(v.reshape(v.shape[0], HEADS_HERE, HD), 1, 0)


def join_heads(v):
    return jnp.moveaxis(v, 0, 1).reshape(v.shape[1], HEADS_HERE * HD)


def attend_forward(queries, keys, values, allowed, live):
    scores = jnp.einsum("hqe,hke->hqk", queries, keys, preferred_element_type=F32) * HD**-0.5
    masked = jnp.where(allowed, scores, -1e30)
    highest = jnp.max(masked, axis=-1, keepdims=True)
    exponent = jnp.exp(masked - highest)
    totals = jnp.sum(exponent, axis=-1, keepdims=True)
    probs = (exponent / totals).astype(BF)
    heads = jnp.einsum("hqk,hke->hqe", probs, values, preferred_element_type=F32)
    return (heads * live[:, None, None]).astype(BF), highest + jnp.log(totals)


def attend_backward(queries, keys, values, log_total, grad_heads, allowed):
    scores = jnp.einsum("hqe,hke->hqk", queries, keys, preferred_element_type=F32) * HD**-0.5
    probs = jnp.exp(jnp.where(allowed, scores, -1e30) - log_total)
    grad_probs = jnp.einsum("hqe,hke->hqk", grad_heads, values, preferred_element_type=F32)
    centred = grad_probs - jnp.sum(grad_probs * probs, axis=-1, keepdims=True)
    grad_scores = (probs * centred).astype(BF)
    grad_q = jnp.einsum("hqk,hke->hqe", grad_scores, keys, preferred_element_type=F32)
    grad_k = jnp.einsum("hqk,hqe->hke", grad_scores, queries, preferred_element_type=F32)
    grad_v = jnp.einsum("hqk,hqe->hke", probs.astype(BF), grad_heads, preferred_element_type=F32)
    return (
        (grad_q * HD**-0.5).astype(BF),
        (grad_k * HD**-0.5).astype(BF),
        grad_v.astype(BF),
    )


def heads_first(w_qkv, w_out, h):
    first, count = (0, 3) if h == 0 else (3, 2)
    picked = jnp.moveaxis(w_qkv[first : first + count], 0, 1)
    outs = jnp.moveaxis(w_out[first : first + count], 2, 0)
    cols = [picked[:, :, i * HD : (i + 1) * HD] for i in range(3)] + [outs]
    cols = [jnp.pad(a, ((0, 0), (0, HEADS_HERE - count), (0, 0))) for a in cols]
    return jnp.concatenate([a.reshape(CHUNK, QW) for a in cols], axis=1)


def hidden_first(w_fc, w_down, h):
    gap = ((0, 0), (0, FP - FH))
    return jnp.concatenate(
        [
            jnp.pad(w_fc[:, h * FH : (h + 1) * FH], gap),
            jnp.pad(w_down[h * FH : (h + 1) * FH].T, gap),
        ],
        axis=1,
    )


def shards(
    tokens,
    cotangent,
    block_order,
    head_count,
    ln_gain,
    ln_bias,
    w_qkv,
    b_qv,
    w_out,
    b_out,
    w_fc,
    b_fc,
    w_down,
    b_down,
):
    ctx = lax.axis_index("ctx")
    tp = lax.axis_index("tp")
    first = ctx == 0

    wide = jnp.arange(DP, dtype=jnp.int32)
    inside = wide % WIDE
    source = jnp.where(inside < CHUNK, wide // WIDE * CHUNK + inside, -1)
    spread = (source[None, :] == jnp.arange(D, dtype=jnp.int32)[:, None]).astype(BF)
    mask = (inside < CHUNK).astype(F32)[None, :]

    def widen(v):
        full = v.reshape(-1, D)
        out = lax.dot_general(
            full,
            spread.astype(full.dtype),
            (((1,), (0,)), ((), ())),
            precision=lax.Precision.HIGHEST if full.dtype == F32 else None,
            preferred_element_type=F32,
        )
        return out.reshape(*v.shape[:-1], DP)

    def narrow(v):
        return lax.dot_general(
            v,
            spread.astype(v.dtype),
            (((1,), (1,)), ((), ())),
            precision=lax.Precision.HIGHEST if v.dtype == F32 else None,
            preferred_element_type=F32,
        )

    def exchanged(halves):
        keep = jnp.where(first, halves[0], halves[1])
        send = jnp.where(first, halves[1], halves[0])
        recv = swap_ctx(send)
        top = jnp.where(first, keep, recv)
        low = jnp.where(first, recv, keep)
        gap = ((0, WIDE - CHUNK), (0, 0))
        return jnp.concatenate([jnp.pad(top, gap), jnp.pad(low, gap)], axis=0)

    packs = []
    for l in range(LAYERS):
        packs.append(
            (
                exchanged([heads_first(w_qkv[l, 0], w_out[l, 0], h) for h in range(2)]),
                exchanged([hidden_first(w_fc[l], w_down[l], h) for h in range(2)]),
            )
        )

    def fetch(pack):
        return lax.all_gather(pack, "shard", axis=0, tiled=True)

    weights = [(fetch(a), fetch(b)) for a, b in packs]

    core = tp % 2
    x = (tp // 2) * 2 + ctx
    units = []
    for j in range(2):
        for m in range(4):
            chip = x ^ m
            block = (chip % 2) * 2 + chip // 2
            start = jnp.sum(jnp.where(jnp.arange(4) == block, block_order, 0)) * 256
            units.append(start + (core ^ j) * ROWS + jnp.arange(ROWS, dtype=jnp.int32))
    places = jnp.concatenate(units)
    allowed = places[None, :] <= places[:, None]
    my_count = jnp.sum(jnp.where(jnp.arange(4) == tp, head_count, 0))
    slot = jnp.arange(HEADS_HERE, dtype=jnp.int32) + ctx * HEADS_HERE
    live = ((slot < my_count) & (slot < 5)).astype(F32)

    head_bias = jnp.pad(b_qv[:, 0], ((0, 0), (0, 1), (0, 0)))
    head_bias = jnp.where(first, head_bias[:, :3], head_bias[:, 3:])
    q_bias = head_bias[:, :, :HD].reshape(LAYERS, QW)
    v_bias = head_bias[:, :, HD:].reshape(LAYERS, QW)
    fc_bias = jnp.where(first, b_fc[:, :FH], b_fc[:, FH:])

    vectors = widen(
        jnp.concatenate([ln_gain.reshape(4, D), ln_bias.reshape(4, D), b_out, b_down], axis=0)
    )
    gains = vectors[0:4].reshape(LAYERS, 2, DP)
    shifts = vectors[4:8].reshape(LAYERS, 2, DP)
    out_bias, down_bias = vectors[8:10], vectors[10:12]

    hidden = widen(tokens[0])
    gradient = widen(cotangent[0])
    stored = []
    for l in range(LAYERS):
        w_heads, w_hidden = weights[l]
        normed, xhat, rstd = norm_forward(hidden, gains[l, 0], shifts[l, 0], mask)
        normed_all = gather_rows(normed)
        projected = dot(normed_all, w_heads[:, : 3 * QW], ((1,), (0,)))
        queries = split_heads((projected[:, :QW] + q_bias[l]).astype(BF))
        keys = split_heads(projected[:, QW : 2 * QW].astype(BF))
        values = split_heads((projected[:, 2 * QW :] + v_bias[l]).astype(BF))
        attended, log_total = attend_forward(queries, keys, values, allowed, live)
        attended = join_heads(attended)
        mixed_out = dot(attended, w_heads[:, 3 * QW :], ((1,), (1,)))
        middle = hidden + (sum_rows(mixed_out) + out_bias[l])
        normed_two, xhat_two, rstd_two = norm_forward(middle, gains[l, 1], shifts[l, 1], mask)
        normed_two_all = gather_rows(normed_two)
        inner = dot(normed_two_all, w_hidden[:, :FH], ((1,), (0,))) + fc_bias[l]
        activated = gelu_exact(inner).astype(BF)
        down_out = dot(activated, w_hidden[:, FP : FP + FH], ((1,), (1,)))
        hidden = middle + (sum_rows(down_out) + down_bias[l])
        stored.append(
            (
                normed_all,
                xhat,
                rstd,
                queries,
                keys,
                values,
                log_total,
                attended,
                normed_two_all,
                xhat_two,
                rstd_two,
                inner,
                activated,
            )
        )
    mixed = narrow(hidden.astype(BF)).astype(BF)

    small = [None] * LAYERS
    biases = [None] * LAYERS
    head_sums = [None] * LAYERS
    hidden_sums = [None] * LAYERS

    def to_owner(v):
        return lax.psum_scatter(v, "shard", scatter_dimension=0, tiled=True)

    for l in reversed(range(LAYERS)):
        w_heads, w_hidden = weights[l]
        (
            normed_all,
            xhat,
            rstd,
            queries,
            keys,
            values,
            log_total,
            attended,
            normed_two_all,
            xhat_two,
            rstd_two,
            inner,
            activated,
        ) = stored[l]
        g_low = gradient.astype(BF)
        g_all = gather_rows(g_low)
        grad_down_b = jnp.sum(g_low.astype(F32), axis=0)
        grad_down_w = dot(g_all, activated, ((0,), (0,))).astype(BF)
        grad_activated = dot(g_all, w_hidden[:, FP : FP + FH], ((1,), (0,)))
        grad_inner = jax.vjp(gelu_exact, inner)[1](grad_activated)[0].astype(BF)
        grad_fc_w = dot(normed_two_all, grad_inner, ((0,), (0,))).astype(BF)
        grad_fc_b = jnp.sum(grad_inner.astype(F32), axis=0)
        grad_two = sum_rows(dot(grad_inner, w_hidden[:, :FH], ((1,), (1,))))
        dx, gain_two, shift_two = norm_backward(grad_two, xhat_two, rstd_two, gains[l, 1], mask)
        grad_middle = gradient + dx
        m_low = grad_middle.astype(BF)
        m_all = gather_rows(m_low)
        grad_out_b = jnp.sum(m_low.astype(F32), axis=0)
        grad_out_w = dot(m_all, attended, ((0,), (0,))).astype(BF)
        gap = ((0, 0), (0, FP - FH))
        hidden_sums[l] = to_owner(
            jnp.concatenate(
                [jnp.pad(grad_fc_w, gap), jnp.pad(grad_down_w, gap), grad_out_w], axis=1
            )
        )
        grad_heads = split_heads(dot(m_all, w_heads[:, 3 * QW :], ((1,), (0,))).astype(BF))
        grad_heads = grad_heads * live[:, None, None].astype(BF)
        grad_q, grad_k, grad_v = attend_backward(
            queries, keys, values, log_total, grad_heads, allowed
        )
        grad_qkv = jnp.concatenate([join_heads(a) for a in (grad_q, grad_k, grad_v)], axis=1)
        head_sums[l] = to_owner(dot(normed_all, grad_qkv, ((0,), (0,))).astype(BF))
        qkv_b = jnp.sum(grad_qkv.astype(F32), axis=0)
        grad_one = sum_rows(dot(grad_qkv, w_heads[:, : 3 * QW], ((1,), (1,))))
        dx, gain_one, shift_one = norm_backward(grad_one, xhat, rstd, gains[l, 0], mask)
        gradient = grad_middle + dx
        small[l] = [gain_one, gain_two, shift_one, shift_two, grad_out_b, grad_down_b]
        biases[l] = jnp.pad(
            jnp.concatenate([grad_fc_b, qkv_b[:QW], qkv_b[2 * QW :]]), (0, DP - FH - 2 * QW)
        )

    line = sum_line(jnp.stack(small[0] + small[1]))
    own = jnp.stack(biases)
    other = swap_ctx(own)
    both = jnp.concatenate([jnp.where(first, own, other), jnp.where(first, other, own)], axis=0)
    sums = sum_shards(jnp.concatenate([line, both], axis=0))
    vectors = narrow(sums[:12]).reshape(LAYERS, 6, D)
    halves = sums[12:].reshape(2, LAYERS, DP)
    fc_sum = jnp.concatenate([halves[0, :, :FH], halves[1, :, :FH]], axis=1)

    def slots_of(v):
        v = v.reshape(2, LAYERS, HEADS_HERE, HD)
        return jnp.concatenate([v[0], v[1, :, :2]], axis=1)

    head_sum = jnp.concatenate(
        [slots_of(halves[:, :, FH : FH + QW]), slots_of(halves[:, :, FH + QW : FH + 2 * QW])],
        axis=-1,
    )

    def own_features(v):
        keep = jnp.where(first, v[:WIDE], v[WIDE:])
        recv = swap_ctx(jnp.where(first, v[WIDE:], v[:WIDE]))
        return (
            jnp.where(first, keep, recv)[:CHUNK].astype(F32),
            jnp.where(first, recv, keep)[:CHUNK].astype(F32),
        )

    grads = [[], [], [], []]
    for l in range(LAYERS):
        a, b = own_features(head_sums[l])

        def slot_major(v, count):
            return jnp.transpose(v.reshape(CHUNK, 3, HEADS_HERE, HD)[:, :, :count], (2, 0, 1, 3))

        qkv = jnp.concatenate([slot_major(a, 3), slot_major(b, 2)], axis=0)
        grads[0].append(qkv.reshape(5, CHUNK, 3 * HD))
        a, b = own_features(hidden_sums[l])
        outs = jnp.concatenate([a[:, 2 * FP :], b[:, 2 * FP : 2 * FP + 2 * HD]], axis=1)
        grads[1].append(outs.T.reshape(5, HD, CHUNK))
        grads[2].append(jnp.concatenate([a[:, :FH], b[:, :FH]], axis=1))
        grads[3].append(jnp.concatenate([a[:, FP : FP + FH], b[:, FP : FP + FH]], axis=1).T)

    return (
        mixed[None],
        narrow(gradient)[None],
        vectors[:, 0:2],
        vectors[:, 2:4],
        jnp.stack(grads[0])[:, None],
        head_sum[:, None],
        jnp.stack(grads[1])[:, None],
        vectors[:, 4],
        jnp.stack(grads[2]),
        fc_sum,
        jnp.stack(grads[3]),
        vectors[:, 5],
    )


def solution(mesh):
    in_specs = (
        P("shard", ("ctx", "tp"), None),
        P("shard", ("ctx", "tp"), None),
        P(),
        P(),
        P(),
        P(),
        P(None, "tp", None, ("shard", "ctx"), None),
        P(None, "tp", None, None),
        P(None, "tp", None, None, ("shard", "ctx")),
        P(),
        P(None, ("shard", "ctx"), "tp"),
        P(None, "tp"),
        P(None, "tp", ("shard", "ctx")),
        P(),
    )
    out_specs = (
        P("shard", ("ctx", "tp"), None),
        P("shard", ("ctx", "tp"), None),
        P(),
        P(),
        P(None, "tp", None, ("shard", "ctx"), None),
        P(None, "tp", None, None),
        P(None, "tp", None, None, ("shard", "ctx")),
        P(),
        P(None, ("shard", "ctx"), "tp"),
        P(None, "tp"),
        P(None, "tp", ("shard", "ctx")),
        P(),
    )
    return jax.shard_map(shards, mesh=mesh, in_specs=in_specs, out_specs=out_specs, check_vma=False)
```

```python
import jax
import jax.numpy as jnp
from jax import lax
from jax.experimental import pallas as pl
from jax.experimental.pallas import tpu as pltpu
from jax.sharding import PartitionSpec as P

D = 1088
HD = 64
LAYERS = 2
EPS = 1e-05
SHARDS = 16
CHUNK = 34
WIDE = 36
DP = 2 * SHARDS * WIDE
HEADS_HERE = 3
QW = HEADS_HERE * HD
FR = 1088
FC = 2 * FR
HW = 4 * QW
ROWS = 128
BF = jnp.bfloat16
F32 = jnp.float32
LINE = ("ctx", "tp")


def line_perm(target):
    pairs = []
    for c in range(2):
        for h in range(2):
            for k in range(2):
                x2, k2 = target(2 * h + c, k)
                pairs.append((c * 4 + h * 2 + k, (x2 % 2) * 4 + (x2 // 2) * 2 + k2))
    return pairs


def swap_core(v):
    return lax.ppermute(v, LINE, line_perm(lambda x, k: (x, 1 - k)))


def swap_x(v, m):
    return lax.ppermute(v, LINE, line_perm(lambda x, k: (x ^ m, k)))


def swap_ctx(v):
    return lax.ppermute(v, "ctx", [(0, 1), (1, 0)])


def swap_shard(v, m):
    return lax.ppermute(v, "shard", [(i, i ^ m) for i in range(SHARDS)])


def ordered(parts, place):
    odd, high = place % 2 == 1, place // 2 == 1
    parts = [jnp.where(odd, parts[i ^ 1], parts[i]) for i in range(4)]
    return jnp.concatenate([jnp.where(high, parts[i ^ 2], parts[i]) for i in range(4)], axis=0)


def gather_shards(v):
    shard = lax.axis_index("shard")
    v = ordered([v] + [swap_shard(v, m) for m in (1, 2, 3)], shard % 4)
    return ordered([v] + [swap_shard(v, 4 * m) for m in (1, 2, 3)], shard // 4)


def to_shards(v):
    shard = lax.axis_index("shard")

    def stage(v, axis, step):
        place = shard // step % 4

        def part(m):
            return lax.dynamic_index_in_dim(v, place ^ m, axis, keepdims=False)

        came = [swap_shard(part(m).astype(BF), m * step).astype(F32) for m in (1, 2, 3)]
        return (part(0).astype(F32) + came[0]) + (came[1] + came[2])

    v = v.reshape(4, 4, v.shape[0] // SHARDS, v.shape[1])
    half = v.shape[3] // 2
    a = stage(stage(v[..., :half], 1, 1), 0, 4)
    b = stage(stage(v[..., half:], 0, 4), 0, 1)
    return jnp.concatenate([a, b], axis=1)


def gather_pair(piece):
    return jnp.concatenate([piece, swap_core(piece)], axis=0)


def sum_pair(partial):
    return partial[:ROWS] + swap_core(partial[ROWS:].astype(BF)).astype(F32)


def gather_rows(piece):
    mine = jnp.concatenate([piece] + [swap_x(piece, m) for m in (1, 2, 3)], axis=0)
    return jnp.concatenate([mine, swap_core(mine)], axis=0)


def sum_rows(partial):
    half = 4 * ROWS
    arrived = swap_core(partial[half:].astype(BF))
    chip = partial[:half] + arrived.astype(F32)
    low = chip.astype(BF)
    parts = [swap_x(low[m * ROWS : (m + 1) * ROWS], m).astype(F32) for m in (1, 2, 3)]
    return (chip[:ROWS] + parts[0]) + (parts[1] + parts[2])


def sum_shards(v):
    v = (v + swap_shard(v, 1)) + (swap_shard(v, 2) + swap_shard(v, 3))
    return (v + swap_shard(v, 4)) + (swap_shard(v, 8) + swap_shard(v, 12))


def sum_line_parts(both_cores, each_core):
    v = jnp.concatenate([both_cores + swap_core(both_cores), each_core], axis=0)
    return (v + swap_x(v, 1)) + (swap_x(v, 2) + swap_x(v, 3))


def dot(a, b, dims):
    return lax.dot_general(a, b, (dims, ((), ())), preferred_element_type=F32)


def norm_forward(x, gain, shift, mask):
    mean = jnp.sum(x, axis=-1, keepdims=True) * (1.0 / D)
    centred = (x - mean) * mask
    var = jnp.sum(centred * centred, axis=-1, keepdims=True) * (1.0 / D)
    rstd = lax.rsqrt(var + EPS)
    xhat = centred * rstd
    return (xhat * gain + shift).astype(BF), xhat, rstd


def norm_backward(dy, xhat, rstd, gain, mask):
    e = dy * gain
    mean_e = jnp.sum(e, axis=-1, keepdims=True) * (1.0 / D)
    mean_ex = jnp.sum(e * xhat, axis=-1, keepdims=True) * (1.0 / D)
    dx = rstd * (e - mean_e - xhat * mean_ex) * mask
    return dx, jnp.sum(dy * xhat, axis=0), jnp.sum(dy, axis=0)


def gelu_exact(v):
    return jax.nn.gelu(v, approximate=False)


def split_heads(v):
    parts = v.shape[1] // QW
    v = v.reshape(v.shape[0], HEADS_HERE, parts, HD)
    return [jnp.moveaxis(v[:, :, i], 1, 0) for i in range(parts)]


def join_heads(*parts):
    v = jnp.stack(parts, axis=2)
    return jnp.moveaxis(v, 0, 1).reshape(v.shape[1], -1)


def attend_forward(queries, keys, values, allowed, live):
    scores = jnp.einsum("hqe,hke->hqk", queries, keys, preferred_element_type=F32) * HD**-0.5
    masked = jnp.where(allowed, scores, -1e30)
    highest = jnp.max(masked, axis=-1, keepdims=True)
    exponent = jnp.exp(masked - highest)
    totals = jnp.sum(exponent, axis=-1, keepdims=True)
    probs = (exponent / totals).astype(BF)
    heads = jnp.einsum("hqk,hke->hqe", probs, values, preferred_element_type=F32)
    return (heads * live[:, None, None]).astype(BF), highest + jnp.log(totals)


def attend_backward(queries, keys, values, log_total, grad_heads, allowed):
    scores = jnp.einsum("hqe,hke->hqk", queries, keys, preferred_element_type=F32) * HD**-0.5
    probs = jnp.exp(jnp.where(allowed, scores, -1e30) - log_total)
    grad_probs = jnp.einsum("hqe,hke->hqk", grad_heads, values, preferred_element_type=F32)
    centred = grad_probs - jnp.sum(grad_probs * probs, axis=-1, keepdims=True)
    grad_scores = (probs * centred).astype(BF)
    grad_q = jnp.einsum("hqk,hke->hqe", grad_scores, keys, preferred_element_type=F32)
    grad_k = jnp.einsum("hqk,hqe->hke", grad_scores, queries, preferred_element_type=F32)
    grad_v = jnp.einsum("hqk,hqe->hke", probs.astype(BF), grad_heads, preferred_element_type=F32)
    return (
        (grad_q * HD**-0.5).astype(BF),
        (grad_k * HD**-0.5).astype(BF),
        grad_v.astype(BF),
    )


def head_halves(w_qkv, w_out):
    cols = jnp.moveaxis(w_qkv, 0, 1).reshape(CHUNK, 15 * HD)
    outs = w_out.reshape(5 * HD, CHUNK).T
    gap = ((0, 0), (0, HD))
    return (
        jnp.concatenate([cols[:, : 3 * QW], outs[:, :QW]], axis=1),
        jnp.concatenate(
            [jnp.pad(cols[:, 3 * QW :], ((0, 0), (0, QW))), jnp.pad(outs[:, QW:], gap)], axis=1
        ),
    )


GRAD_ROWS = 384


def hidden_grads_body(heads, x_ref, dinner_ref, g_ref, act_ref, *refs):
    out_ref = refs[-1]
    turned = (((0,), (0,)), ((), ()))
    out_ref[:, :FC] = lax.dot_general(
        x_ref[...], dinner_ref[...], turned, preferred_element_type=F32
    ).astype(BF)
    out_ref[:, FC : 2 * FC] = lax.dot_general(
        g_ref[...], act_ref[...], turned, preferred_element_type=F32
    ).astype(BF)
    if heads:
        out_ref[:, 2 * FC :] = refs[0][...]


def hidden_grads(x, dinner, g, act, head_grads=None):
    rows = x.shape[0]
    wide = 2 * FC + (0 if head_grads is None else HW)
    args = [x, dinner, g, act] + ([] if head_grads is None else [head_grads])
    feature = pl.BlockSpec((rows, GRAD_ROWS), lambda i: (0, i))
    whole = pl.BlockSpec((rows, FC), lambda i: (0, 0))
    specs = [feature, whole, feature, whole]
    if head_grads is not None:
        specs.append(pl.BlockSpec((GRAD_ROWS, HW), lambda i: (i, 0)))
    return pl.pallas_call(
        lambda *refs: hidden_grads_body(head_grads is not None, *refs),
        grid=(DP // GRAD_ROWS,),
        in_specs=specs,
        out_specs=pl.BlockSpec((GRAD_ROWS, wide), lambda i: (i, 0)),
        out_shape=jax.ShapeDtypeStruct((DP, wide), BF),
        compiler_params=pltpu.CompilerParams(vmem_limit_bytes=48 << 20),
        cost_estimate=pl.CostEstimate(
            flops=4 * rows * DP * FC, bytes_accessed=2 * DP * wide, transcendentals=0
        ),
        name="hidden_grads",
    )(*args)


def shards(
    tokens,
    cotangent,
    block_order,
    head_count,
    ln_gain,
    ln_bias,
    w_qkv,
    b_qv,
    w_out,
    b_out,
    w_fc,
    b_fc,
    w_down,
    b_down,
):
    ctx = lax.axis_index("ctx")
    tp = lax.axis_index("tp")
    first = ctx == 0

    wide = jnp.arange(DP, dtype=jnp.int32)
    inside = wide % WIDE
    source = jnp.where(inside < CHUNK, wide // WIDE * CHUNK + inside, -1)
    spread = (source[None, :] == jnp.arange(D, dtype=jnp.int32)[:, None]).astype(BF)
    mask = (inside < CHUNK).astype(F32)[None, :]

    def widen(v):
        full = v.reshape(-1, D)
        out = lax.dot_general(
            full,
            spread.astype(full.dtype),
            (((1,), (0,)), ((), ())),
            precision=lax.Precision.HIGHEST if full.dtype == F32 else None,
            preferred_element_type=F32,
        )
        return out.reshape(*v.shape[:-1], DP)

    def narrow(v):
        return lax.dot_general(
            v,
            spread.astype(v.dtype),
            (((1,), (1,)), ((), ())),
            precision=lax.Precision.HIGHEST if v.dtype == F32 else None,
            preferred_element_type=F32,
        )

    def exchanged(halves):
        keep = jnp.where(first, halves[0], halves[1])
        send = jnp.where(first, halves[1], halves[0])
        recv = swap_ctx(send)
        top = jnp.where(first, keep, recv)
        low = jnp.where(first, recv, keep)
        gap = ((0, WIDE - CHUNK), (0, 0))
        return jnp.concatenate([jnp.pad(top, gap), jnp.pad(low, gap)], axis=0)

    def exchanged_hidden(w_fc, w_down):
        raw = jnp.concatenate([w_fc, w_down.T], axis=1)
        raw = jnp.pad(raw, ((0, WIDE - CHUNK), (0, 0)))
        p = [raw] + [swap_x(raw, m) for m in (1, 2, 3)]
        own, other = [
            jnp.concatenate([jnp.where(first, a, b), jnp.where(first, b, a)], axis=0)
            for a, b in ((p[0], p[1]), (p[2], p[3]))
        ]
        return jnp.concatenate([own[:, :FR], other[:, :FR], own[:, FR:], other[:, FR:]], axis=1)

    def fetch(pack):
        return lax.all_gather(pack, "shard", axis=0, tiled=True)

    halves_a = head_halves(w_qkv[0, 0], w_out[0, 0])
    pack_a = exchanged(halves_a)
    w_fc_a, w_down_a, w_qkv_b, w_out_b, pack_a = lax.optimization_barrier(
        (w_fc[0], w_down[0], w_qkv[1, 0], w_out[1, 0], pack_a)
    )
    hidden_a = exchanged_hidden(w_fc_a, w_down_a)
    heads_b = exchanged(head_halves(w_qkv_b, w_out_b))
    fetched_a = fetch(jnp.concatenate([hidden_a, heads_b], axis=1))
    weights = [
        (gather_shards(pack_a), fetched_a[:, : 2 * FC]),
        (fetched_a[:, 2 * FC :], None),
    ]

    core = tp % 2
    x = (tp // 2) * 2 + ctx
    units = []
    for j in range(2):
        for m in range(4):
            chip = x ^ m
            block = (chip % 2) * 2 + chip // 2
            start = jnp.sum(jnp.where(jnp.arange(4) == block, block_order, 0)) * 256
            units.append(start + (core ^ j) * ROWS + jnp.arange(ROWS, dtype=jnp.int32))
    places = jnp.concatenate(units)
    allowed = places[None, :] <= places[:, None]
    my_count = jnp.sum(jnp.where(jnp.arange(4) == tp, head_count, 0))
    slot = jnp.arange(HEADS_HERE, dtype=jnp.int32) + ctx * HEADS_HERE
    live = ((slot < my_count) & (slot < 5)).astype(F32)

    head_bias = jnp.pad(b_qv[:, 0], ((0, 0), (0, 1), (0, 0)))
    head_bias = jnp.where(first, head_bias[:, :3], head_bias[:, 3:])
    head_bias = jnp.concatenate(
        [head_bias[..., :HD], jnp.zeros_like(head_bias[..., :HD]), head_bias[..., HD:]], axis=-1
    ).reshape(LAYERS, 3 * QW)
    fc_bias = jnp.concatenate([b_fc, swap_x(b_fc, 2)], axis=1)

    vectors = widen(
        jnp.concatenate([ln_gain.reshape(4, D), ln_bias.reshape(4, D), b_out, b_down], axis=0)
    )
    gains = vectors[0:4].reshape(LAYERS, 2, DP)
    shifts = vectors[4:8].reshape(LAYERS, 2, DP)
    out_bias, down_bias = vectors[8:10], vectors[10:12]

    hidden = widen(tokens[0])
    gradient = widen(cotangent[0])
    stored = []
    for l in range(LAYERS):
        w_heads, w_hidden = weights[l]
        normed, xhat, rstd = norm_forward(hidden, gains[l, 0], shifts[l, 0], mask)
        normed_all = gather_rows(normed)
        if l == 0:
            normed_all, w_fc_b, w_down_b = lax.optimization_barrier(
                (normed_all, w_fc[1], w_down[1])
            )
            weights[1] = (weights[1][0], fetch(exchanged_hidden(w_fc_b, w_down_b)))
        projected = dot(normed_all, w_heads[:, : 3 * QW], ((1,), (0,)))
        queries, keys, values = split_heads((projected + head_bias[l]).astype(BF))
        attended, log_total = attend_forward(queries, keys, values, allowed, live)
        attended = join_heads(attended)
        mixed_out = dot(attended, w_heads[:, 3 * QW :], ((1,), (1,)))
        middle = hidden + (sum_rows(mixed_out) + out_bias[l])
        normed_two, xhat_two, rstd_two = norm_forward(middle, gains[l, 1], shifts[l, 1], mask)
        normed_two_all = gather_pair(normed_two)
        inner = dot(normed_two_all, w_hidden[:, :FC], ((1,), (0,))) + fc_bias[l]
        activated = gelu_exact(inner).astype(BF)
        down_out = dot(activated, w_hidden[:, FC:], ((1,), (1,)))
        hidden = middle + (sum_pair(down_out) + down_bias[l])
        stored.append(
            (
                normed_all,
                xhat,
                rstd,
                queries,
                keys,
                values,
                log_total,
                attended,
                normed_two_all,
                xhat_two,
                rstd_two,
                inner,
                activated,
            )
        )
    mixed = narrow(hidden.astype(BF)).astype(BF)

    small = [None] * LAYERS
    fc_biases, head_biases = [], []
    high = tp // 2 == 1
    hidden_sums = [None] * LAYERS

    def to_owner(v, dim):
        v = v.reshape((1,) * dim + v.shape)
        v = lax.psum_scatter(v, "shard", scatter_dimension=dim, tiled=True)
        return lax.optimization_barrier(v).reshape(v.shape[-2:])

    for l in reversed(range(LAYERS)):
        w_heads, w_hidden = weights[l]
        (
            normed_all,
            xhat,
            rstd,
            queries,
            keys,
            values,
            log_total,
            attended,
            normed_two_all,
            xhat_two,
            rstd_two,
            inner,
            activated,
        ) = stored[l]
        g_low = gradient.astype(BF)
        g_all = gather_pair(g_low)
        grad_down_b = jnp.sum(g_low.astype(F32), axis=0)
        grad_activated = dot(g_all, w_hidden[:, FC:], ((1,), (0,)))
        grad_inner = jax.vjp(gelu_exact, inner)[1](grad_activated)[0].astype(BF)
        grad_fc_b = jnp.sum(grad_inner.astype(F32), axis=0)
        hidden_sums[l] = to_owner(
            hidden_grads(
                normed_two_all, grad_inner, g_all, activated, head_grads if l == 0 else None
            ),
            1 - l,
        )
        grad_two = sum_pair(dot(grad_inner, w_hidden[:, :FC], ((1,), (1,))))
        dx, gain_two, shift_two = norm_backward(grad_two, xhat_two, rstd_two, gains[l, 1], mask)
        grad_middle = gradient + dx
        m_low = grad_middle.astype(BF)
        m_all = gather_rows(m_low)
        grad_out_b = jnp.sum(m_low.astype(F32), axis=0)
        grad_out_w = dot(m_all, attended, ((0,), (0,))).astype(BF)
        (grad_heads,) = split_heads(dot(m_all, w_heads[:, 3 * QW :], ((1,), (0,))).astype(BF))
        grad_heads = grad_heads * live[:, None, None].astype(BF)
        grad_q, grad_k, grad_v = attend_backward(
            queries, keys, values, log_total, grad_heads, allowed
        )
        grad_qkv = join_heads(grad_q, grad_k, grad_v)
        grad_qkv_w = dot(normed_all, grad_qkv, ((0,), (0,))).astype(BF)
        head_grads = jnp.concatenate([grad_qkv_w, grad_out_w], axis=1)
        qkv_b = jnp.sum(grad_qkv.astype(F32), axis=0)
        grad_one = sum_rows(dot(grad_qkv, w_heads[:, : 3 * QW], ((1,), (1,))))
        dx, gain_one, shift_one = norm_backward(grad_one, xhat, rstd, gains[l, 0], mask)
        gradient = grad_middle + dx
        small[l] = [gain_one, gain_two, shift_one, shift_two, grad_out_b, grad_down_b]
        fc_biases.append(
            jnp.where(high, jnp.roll(grad_fc_b, FR), grad_fc_b)
        )
        head_biases.append(qkv_b)

    line = sum_line_parts(
        jnp.stack(small[0] + small[1]),
        jnp.pad(jnp.stack(fc_biases[::-1]), ((0, 0), (0, 2 * DP - FC))).reshape(4, DP),
    )
    own = jnp.pad(jnp.stack(head_biases[::-1]), ((0, 0), (0, DP - 3 * QW)))
    other = swap_ctx(own)
    both = jnp.concatenate([jnp.where(first, own, other), jnp.where(first, other, own)], axis=0)
    sums = sum_shards(jnp.concatenate([line, both], axis=0))
    vectors = narrow(sums[:12]).reshape(LAYERS, 6, D)
    fc_sum = sums[12:16].reshape(LAYERS, 2 * DP)
    fc_sum = jnp.where(high, fc_sum[:, FR : 2 * FR], fc_sum[:, :FR])
    halves = sums[16:].reshape(2, LAYERS, DP)[:, :, : 3 * QW].reshape(2, LAYERS, 3, 3, HD)
    head_sum = jnp.concatenate([halves[0], halves[1, :, :2]], axis=1)
    head_sum = jnp.concatenate([head_sum[:, :, 0], head_sum[:, :, 2]], axis=-1)

    def own_features(v):
        keep = jnp.where(first, v[:WIDE], v[WIDE:])
        recv = swap_ctx(jnp.where(first, v[WIDE:], v[:WIDE]))
        return (
            jnp.where(first, keep, recv)[:CHUNK].astype(F32),
            jnp.where(first, recv, keep)[:CHUNK].astype(F32),
        )

    def own_hidden(v):
        mine = jnp.where(first, v[:WIDE], v[WIDE:])
        theirs = jnp.where(first, v[WIDE:], v[:WIDE])

        def piece(rows, h):
            return jnp.concatenate(
                [rows[:, h * FR : (h + 1) * FR], rows[:, FC + h * FR : FC + (h + 1) * FR]], axis=1
            )

        came = [swap_x(piece(theirs if m % 2 else mine, m // 2), m).astype(F32) for m in (1, 2, 3)]
        return ((piece(mine, 0).astype(F32) + came[0]) + (came[1] + came[2]))[:CHUNK]

    head_sums = [to_shards(head_grads).astype(BF), hidden_sums[0][:, 2 * FC :]]
    grads = [[], [], [], []]
    for l in range(LAYERS):
        a, b = own_features(head_sums[l])
        qkv = jnp.concatenate([a[:, : 3 * QW], b[:, : 2 * QW]], axis=1).reshape(CHUNK, 5, 3 * HD)
        grads[0].append(jnp.moveaxis(qkv, 1, 0))
        outs = jnp.concatenate([a[:, 3 * QW :], b[:, 3 * QW : 3 * QW + 2 * HD]], axis=1)
        grads[1].append(outs.T.reshape(5, HD, CHUNK))
        both = own_hidden(hidden_sums[l][:, : 2 * FC])
        grads[2].append(both[:, :FR])
        grads[3].append(both[:, FR:].T)

    return (
        mixed[None],
        narrow(gradient)[None],
        vectors[:, 0:2],
        vectors[:, 2:4],
        jnp.stack(grads[0])[:, None],
        head_sum[:, None],
        jnp.stack(grads[1])[:, None],
        vectors[:, 4],
        jnp.stack(grads[2]),
        fc_sum,
        jnp.stack(grads[3]),
        vectors[:, 5],
    )


def solution(mesh):
    in_specs = (
        P("shard", ("ctx", "tp"), None),
        P("shard", ("ctx", "tp"), None),
        P(),
        P(),
        P(),
        P(),
        P(None, "tp", None, ("shard", "ctx"), None),
        P(None, "tp", None, None),
        P(None, "tp", None, None, ("shard", "ctx")),
        P(),
        P(None, ("shard", "ctx"), "tp"),
        P(None, "tp"),
        P(None, "tp", ("shard", "ctx")),
        P(),
    )
    out_specs = (
        P("shard", ("ctx", "tp"), None),
        P("shard", ("ctx", "tp"), None),
        P(),
        P(),
        P(None, "tp", None, ("shard", "ctx"), None),
        P(None, "tp", None, None),
        P(None, "tp", None, None, ("shard", "ctx")),
        P(),
        P(None, ("shard", "ctx"), "tp"),
        P(None, "tp"),
        P(None, "tp", ("shard", "ctx")),
        P(),
    )
    return jax.shard_map(shards, mesh=mesh, in_specs=in_specs, out_specs=out_specs, check_vma=False)
```

```python
import jax
import jax.numpy as jnp
from jax import lax
from jax.experimental import pallas as pl
from jax.experimental.pallas import tpu as pltpu
from jax.sharding import PartitionSpec as P

D = 1088
HD = 64
LAYERS = 2
EPS = 1e-05
SHARDS = 16
CHUNK = 34
WIDE = 36
DP = 2 * SHARDS * WIDE
HEADS_HERE = 3
QW = HEADS_HERE * HD
FR = 1088
FC = 2 * FR
HW = 4 * QW
ROWS = 128
BF = jnp.bfloat16
F32 = jnp.float32
LINE = ("ctx", "tp")


def line_perm(target):
    pairs = []
    for c in range(2):
        for h in range(2):
            for k in range(2):
                x2, k2 = target(2 * h + c, k)
                pairs.append((c * 4 + h * 2 + k, (x2 % 2) * 4 + (x2 // 2) * 2 + k2))
    return pairs


def swap_core(v):
    return lax.ppermute(v, LINE, line_perm(lambda x, k: (x, 1 - k)))


def swap_x(v, m):
    return lax.ppermute(v, LINE, line_perm(lambda x, k: (x ^ m, k)))


def swap_ctx(v):
    return lax.ppermute(v, "ctx", [(0, 1), (1, 0)])


def swap_shard(v, m):
    return lax.ppermute(v, "shard", [(i, i ^ m) for i in range(SHARDS)])


def gather_shards(v):
    copies = jnp.broadcast_to(v, (SHARDS, *v.shape))
    return lax.all_to_all(copies, "shard", 0, 0, tiled=True).reshape(-1, v.shape[1])


def to_shards(v):
    v = v.reshape(SHARDS, v.shape[0] // SHARDS, v.shape[1])
    return lax.all_to_all(v, "shard", 0, 0, tiled=True)


def gather_pair(piece):
    return jnp.concatenate([piece, swap_core(piece)], axis=0)


def sum_pair(partial):
    return partial[:ROWS] + swap_core(partial[ROWS:].astype(BF)).astype(F32)


def gather_rows(piece):
    mine = jnp.concatenate([piece] + [swap_x(piece, m) for m in (1, 2, 3)], axis=0)
    return mine, swap_core(mine)


def sum_rows(rows, w, lo, hi):
    arrived = swap_core(dot(rows[HALF:], w[:, lo:hi], ((1,), (1,))).astype(BF))
    own, *others = chip_sum(rows, w, arrived, lo, hi)
    parts = [swap_x(v, m).astype(F32) for m, v in zip((1, 2, 3), others)]
    return (own + parts[0]) + (parts[1] + parts[2])


def sum_shards(v):
    v = (v + swap_shard(v, 1)) + (swap_shard(v, 2) + swap_shard(v, 3))
    return (v + swap_shard(v, 4)) + (swap_shard(v, 8) + swap_shard(v, 12))


def sum_line_parts(both_cores, each_core):
    v = jnp.concatenate([both_cores + swap_core(both_cores), each_core], axis=0)
    return (v + swap_x(v, 1)) + (swap_x(v, 2) + swap_x(v, 3))


def dot(a, b, dims):
    return lax.dot_general(a, b, (dims, ((), ())), preferred_element_type=F32)


def norm_forward(x, gain, shift, mask):
    mean = jnp.sum(x, axis=-1, keepdims=True) * (1.0 / D)
    centred = (x - mean) * mask
    var = jnp.sum(centred * centred, axis=-1, keepdims=True) * (1.0 / D)
    rstd = lax.rsqrt(var + EPS)
    xhat = centred * rstd
    return (xhat * gain + shift).astype(BF), xhat, rstd


def norm_backward(dy, xhat, rstd, gain, mask):
    e = dy * gain
    mean_e = jnp.sum(e, axis=-1, keepdims=True) * (1.0 / D)
    mean_ex = jnp.sum(e * xhat, axis=-1, keepdims=True) * (1.0 / D)
    dx = rstd * (e - mean_e - xhat * mean_ex) * mask
    return dx, jnp.sum(dy * xhat, axis=0), jnp.sum(dy, axis=0)


def gelu_exact(v):
    return jax.nn.gelu(v, approximate=False)


LINE_ROWS = 8 * ROWS
Q_ROWS = 256
PLAIN = (((1,), (0,)), ((), ()))
TURN_RIGHT = (((1,), (1,)), ((), ()))
TURN_LEFT = (((0,), (0,)), ((), ()))


def mul(a, b, dims):
    return lax.dot_general(a, b, dims, preferred_element_type=F32)


def head_parts(ref, rows, j):
    at = 3 * HD * j
    return [ref[rows, at + i * HD : at + (i + 1) * HD] for i in range(3)]


def attend_body(live_ref, kp_ref, qp_ref, qkv_ref, out_ref, lse_ref):
    mine = pl.ds(pl.multiple_of(pl.program_id(0) * Q_ROWS, Q_ROWS), Q_ROWS)
    allowed = kp_ref[...] <= qp_ref[...]
    for j in range(HEADS_HERE):
        queries = qkv_ref[mine, 3 * HD * j : 3 * HD * j + HD]
        _, keys, values = head_parts(qkv_ref, slice(None), j)
        scores = jnp.where(allowed, mul(keys, queries, TURN_RIGHT) * HD**-0.5, -1e30)
        highest = jnp.max(scores, axis=0, keepdims=True)
        exponent = jnp.exp(scores - highest)
        totals = jnp.sum(exponent, axis=0, keepdims=True)
        probs = (exponent * (1.0 / totals)).astype(BF)
        heads = mul(values, probs, TURN_LEFT) * live_ref[j]
        out_ref[:, j * HD : (j + 1) * HD] = heads.T.astype(BF)
        lse_ref[j : j + 1, :] = highest + jnp.log(totals)
    lse_ref[HEADS_HERE:, :] = jnp.zeros((8 - HEADS_HERE, Q_ROWS), F32)


def attend_back_body(
    live_ref, kp_ref, qp_ref, lse_ref, dout_ref, qkv_ref, out_ref, key_sum, value_sum
):
    step = pl.program_id(0)
    mine = pl.ds(pl.multiple_of(step * Q_ROWS, Q_ROWS), Q_ROWS)
    allowed = kp_ref[...] <= qp_ref[...]

    @pl.when(step == 0)
    def _():
        key_sum[...] = jnp.zeros_like(key_sum)
        value_sum[...] = jnp.zeros_like(value_sum)

    for j in range(HEADS_HERE):
        queries = qkv_ref[mine, 3 * HD * j : 3 * HD * j + HD]
        _, keys, values = head_parts(qkv_ref, slice(None), j)
        dout = dout_ref[:, j * HD : (j + 1) * HD] * live_ref[j].astype(BF)
        scores = jnp.where(allowed, mul(keys, queries, TURN_RIGHT) * HD**-0.5, -1e30)
        probs = jnp.exp(scores - lse_ref[j : j + 1, :])
        dprobs = mul(values, dout, TURN_RIGHT)
        dscores = probs * (dprobs - jnp.sum(dprobs * probs, axis=0, keepdims=True))
        dscores = dscores.astype(BF)
        value_sum[j] += mul(probs.astype(BF), dout, PLAIN)
        key_sum[j] += mul(dscores, queries, PLAIN)
        dqueries = mul(keys, dscores, TURN_LEFT) * HD**-0.5
        out_ref[mine, 3 * HD * j : 3 * HD * j + HD] = dqueries.T.astype(BF)

    @pl.when(step == LINE_ROWS // Q_ROWS - 1)
    def _():
        for j in range(HEADS_HERE):
            at = 3 * HD * j
            out_ref[:, at + HD : at + 2 * HD] = (key_sum[j] * HD**-0.5).astype(BF)
            out_ref[:, at + 2 * HD : at + 3 * HD] = value_sum[j].astype(BF)


def attend_specs():
    return [
        pl.BlockSpec(memory_space=pltpu.SMEM),
        pl.BlockSpec((LINE_ROWS, 1), lambda i: (0, 0)),
        pl.BlockSpec((1, Q_ROWS), lambda i: (0, i)),
    ]


def attend_forward(live, places, qkv):
    return pl.pallas_call(
        attend_body,
        grid=(LINE_ROWS // Q_ROWS,),
        in_specs=attend_specs() + [pl.BlockSpec((LINE_ROWS, 3 * QW), lambda i: (0, 0))],
        out_specs=[
            pl.BlockSpec((Q_ROWS, QW), lambda i: (i, 0)),
            pl.BlockSpec((8, Q_ROWS), lambda i: (0, i)),
        ],
        out_shape=[
            jax.ShapeDtypeStruct((LINE_ROWS, QW), BF),
            jax.ShapeDtypeStruct((8, LINE_ROWS), F32),
        ],
        compiler_params=pltpu.CompilerParams(vmem_limit_bytes=48 << 20),
        cost_estimate=pl.CostEstimate(
            flops=4 * HEADS_HERE * LINE_ROWS * LINE_ROWS * HD * 4,
            bytes_accessed=LINE_ROWS * 4 * QW * 2,
            transcendentals=HEADS_HERE * LINE_ROWS * LINE_ROWS,
        ),
        name="attend",
    )(live, places[:, None], places[None, :], qkv)


def attend_backward(live, places, lse, dout, qkv):
    return pl.pallas_call(
        attend_back_body,
        grid=(LINE_ROWS // Q_ROWS,),
        in_specs=attend_specs()
        + [
            pl.BlockSpec((8, Q_ROWS), lambda i: (0, i)),
            pl.BlockSpec((Q_ROWS, QW), lambda i: (i, 0)),
            pl.BlockSpec((LINE_ROWS, 3 * QW), lambda i: (0, 0)),
        ],
        out_specs=pl.BlockSpec((LINE_ROWS, 3 * QW), lambda i: (0, 0)),
        out_shape=jax.ShapeDtypeStruct((LINE_ROWS, 3 * QW), BF),
        scratch_shapes=[pltpu.VMEM((HEADS_HERE, LINE_ROWS, HD), F32)] * 2,
        compiler_params=pltpu.CompilerParams(vmem_limit_bytes=48 << 20),
        cost_estimate=pl.CostEstimate(
            flops=10 * HEADS_HERE * LINE_ROWS * LINE_ROWS * HD * 4,
            bytes_accessed=LINE_ROWS * 7 * QW * 2,
            transcendentals=HEADS_HERE * LINE_ROWS * LINE_ROWS,
        ),
        name="attend_back",
    )(live, places[:, None], places[None, :], lse, dout, qkv)


def head_halves(w_qkv, w_out):
    cols = jnp.moveaxis(w_qkv, 0, 1).reshape(CHUNK, 15 * HD)
    outs = w_out.reshape(5 * HD, CHUNK).T
    gap = ((0, 0), (0, HD))
    return (
        jnp.concatenate([cols[:, : 3 * QW], outs[:, :QW]], axis=1),
        jnp.concatenate(
            [jnp.pad(cols[:, 3 * QW :], ((0, 0), (0, QW))), jnp.pad(outs[:, QW:], gap)], axis=1
        ),
    )


HALF = 4 * ROWS
GRAD_ROWS = 384


def project(pair, w, lo, hi, bias):
    def body(mine, other, w_ref, bias_ref, out_ref):
        for at, x in ((0, mine), (HALF, other)):
            got = mul(x[...], w_ref[:, lo:hi], PLAIN) + bias_ref[...]
            out_ref[at : at + HALF, :] = got.astype(BF)

    return pl.pallas_call(
        body,
        out_shape=jax.ShapeDtypeStruct((2 * HALF, hi - lo), BF),
        compiler_params=pltpu.CompilerParams(vmem_limit_bytes=48 << 20),
        cost_estimate=pl.CostEstimate(
            flops=4 * HALF * DP * (hi - lo), bytes_accessed=8 << 20, transcendentals=0
        ),
        name="project",
    )(*pair, w, bias.reshape(1, hi - lo))


def chip_sum(rows, w, arrived, lo, hi):
    def body(rows_ref, w_ref, arrived_ref, *outs):
        w_part = w_ref[:, lo:hi]
        for m, out in enumerate(outs):
            block = slice(m * ROWS, (m + 1) * ROWS)
            got = mul(rows_ref[block, :], w_part, TURN_RIGHT) + arrived_ref[block, :].astype(F32)
            out[...] = got.astype(out.dtype)

    return pl.pallas_call(
        body,
        grid=(1,),
        in_specs=[
            pl.BlockSpec((HALF, hi - lo), lambda i: (0, 0)),
            pl.BlockSpec((DP, HW), lambda i: (0, 0)),
            pl.BlockSpec((HALF, DP), lambda i: (0, 0)),
        ],
        out_specs=[pl.BlockSpec((ROWS, DP), lambda i: (0, 0))] * 4,
        out_shape=[jax.ShapeDtypeStruct((ROWS, DP), F32 if m == 0 else BF) for m in range(4)],
        compiler_params=pltpu.CompilerParams(vmem_limit_bytes=48 << 20),
        cost_estimate=pl.CostEstimate(
            flops=2 * HALF * DP * (hi - lo), bytes_accessed=6 << 20, transcendentals=0
        ),
        name="chip_sum",
    )(rows, w, arrived)


def head_grads_of(pair, dqkv, m_pair, attended):
    def body(x0, x1, m0, m1, dqkv_ref, att_ref, out_ref):
        got = mul(x0[...], dqkv_ref[:HALF, :], TURN_LEFT)
        got += mul(x1[...], dqkv_ref[HALF:, :], TURN_LEFT)
        out_ref[:, : 3 * QW] = got.astype(BF)
        got = mul(m0[...], att_ref[:HALF, :], TURN_LEFT)
        got += mul(m1[...], att_ref[HALF:, :], TURN_LEFT)
        out_ref[:, 3 * QW :] = got.astype(BF)

    feature = pl.BlockSpec((HALF, GRAD_ROWS), lambda i: (0, i))
    return pl.pallas_call(
        body,
        grid=(DP // GRAD_ROWS,),
        in_specs=[feature] * 4
        + [
            pl.BlockSpec((2 * HALF, 3 * QW), lambda i: (0, 0)),
            pl.BlockSpec((2 * HALF, QW), lambda i: (0, 0)),
        ],
        out_specs=pl.BlockSpec((GRAD_ROWS, HW), lambda i: (i, 0)),
        out_shape=jax.ShapeDtypeStruct((DP, HW), BF),
        compiler_params=pltpu.CompilerParams(vmem_limit_bytes=48 << 20),
        cost_estimate=pl.CostEstimate(
            flops=4 * HALF * DP * HW, bytes_accessed=8 << 20, transcendentals=0
        ),
        name="head_grads",
    )(*pair, *m_pair, dqkv, attended)


def hidden_grads_body(heads, x_ref, dinner_ref, g_ref, act_ref, *refs):
    out_ref = refs[-1]
    turned = (((0,), (0,)), ((), ()))
    out_ref[:, :FC] = lax.dot_general(
        x_ref[...], dinner_ref[...], turned, preferred_element_type=F32
    ).astype(BF)
    out_ref[:, FC : 2 * FC] = lax.dot_general(
        g_ref[...], act_ref[...], turned, preferred_element_type=F32
    ).astype(BF)
    if heads:
        out_ref[:, 2 * FC :] = refs[0][...]


def hidden_grads(x, dinner, g, act, head_grads=None):
    rows = x.shape[0]
    wide = 2 * FC + (0 if head_grads is None else HW)
    args = [x, dinner, g, act] + ([] if head_grads is None else [head_grads])
    feature = pl.BlockSpec((rows, GRAD_ROWS), lambda i: (0, i))
    whole = pl.BlockSpec((rows, FC), lambda i: (0, 0))
    specs = [feature, whole, feature, whole]
    if head_grads is not None:
        specs.append(pl.BlockSpec((GRAD_ROWS, HW), lambda i: (i, 0)))
    return pl.pallas_call(
        lambda *refs: hidden_grads_body(head_grads is not None, *refs),
        grid=(DP // GRAD_ROWS,),
        in_specs=specs,
        out_specs=pl.BlockSpec((GRAD_ROWS, wide), lambda i: (i, 0)),
        out_shape=jax.ShapeDtypeStruct((DP, wide), BF),
        compiler_params=pltpu.CompilerParams(vmem_limit_bytes=48 << 20),
        cost_estimate=pl.CostEstimate(
            flops=4 * rows * DP * FC, bytes_accessed=2 * DP * wide, transcendentals=0
        ),
        name="hidden_grads",
    )(*args)


def shards(
    tokens,
    cotangent,
    block_order,
    head_count,
    ln_gain,
    ln_bias,
    w_qkv,
    b_qv,
    w_out,
    b_out,
    w_fc,
    b_fc,
    w_down,
    b_down,
):
    ctx = lax.axis_index("ctx")
    tp = lax.axis_index("tp")
    first = ctx == 0

    wide = jnp.arange(DP, dtype=jnp.int32)
    inside = wide % WIDE
    source = jnp.where(inside < CHUNK, wide // WIDE * CHUNK + inside, -1)
    spread = (source[None, :] == jnp.arange(D, dtype=jnp.int32)[:, None]).astype(BF)
    mask = (inside < CHUNK).astype(F32)[None, :]

    def widen(v):
        full = v.reshape(-1, D)
        out = lax.dot_general(
            full,
            spread.astype(full.dtype),
            (((1,), (0,)), ((), ())),
            precision=lax.Precision.HIGHEST if full.dtype == F32 else None,
            preferred_element_type=F32,
        )
        return out.reshape(*v.shape[:-1], DP)

    def narrow(v):
        return lax.dot_general(
            v,
            spread.astype(v.dtype),
            (((1,), (1,)), ((), ())),
            precision=lax.Precision.HIGHEST if v.dtype == F32 else None,
            preferred_element_type=F32,
        )

    def exchanged(halves):
        keep = jnp.where(first, halves[0], halves[1])
        send = jnp.where(first, halves[1], halves[0])
        recv = swap_ctx(send)
        top = jnp.where(first, keep, recv)
        low = jnp.where(first, recv, keep)
        gap = ((0, WIDE - CHUNK), (0, 0))
        return jnp.concatenate([jnp.pad(top, gap), jnp.pad(low, gap)], axis=0)

    def exchanged_hidden(w_fc, w_down):
        raw = jnp.concatenate([w_fc, w_down.T], axis=1)
        raw = jnp.pad(raw, ((0, WIDE - CHUNK), (0, 0)))
        p = [raw] + [swap_x(raw, m) for m in (1, 2, 3)]
        own, other = [
            jnp.concatenate([jnp.where(first, a, b), jnp.where(first, b, a)], axis=0)
            for a, b in ((p[0], p[1]), (p[2], p[3]))
        ]
        return jnp.concatenate([own[:, :FR], other[:, :FR], own[:, FR:], other[:, FR:]], axis=1)

    def fetch(pack):
        return lax.all_gather(pack, "shard", axis=0, tiled=True)

    halves_a = head_halves(w_qkv[0, 0], w_out[0, 0])
    pack_a = exchanged(halves_a)
    w_qkv_b, w_out_b, pack_a = lax.optimization_barrier((w_qkv[1, 0], w_out[1, 0], pack_a))
    hidden_a = exchanged_hidden(w_fc[0], w_down[0])
    heads_b = exchanged(head_halves(w_qkv_b, w_out_b))
    heads_a, tokens = lax.optimization_barrier((gather_shards(pack_a), tokens))
    fetched_a = fetch(jnp.concatenate([hidden_a, heads_b], axis=1))
    weights = [
        (heads_a, fetched_a[:, : 2 * FC]),
        (fetched_a[:, 2 * FC :], None),
    ]

    core = tp % 2
    x = (tp // 2) * 2 + ctx
    units = []
    for j in range(2):
        for m in range(4):
            chip = x ^ m
            block = (chip % 2) * 2 + chip // 2
            start = jnp.sum(jnp.where(jnp.arange(4) == block, block_order, 0)) * 256
            units.append(start + (core ^ j) * ROWS + jnp.arange(ROWS, dtype=jnp.int32))
    places = jnp.concatenate(units)
    my_count = jnp.sum(jnp.where(jnp.arange(4) == tp, head_count, 0))
    slot = jnp.arange(HEADS_HERE, dtype=jnp.int32) + ctx * HEADS_HERE
    live = ((slot < my_count) & (slot < 5)).astype(F32)

    head_bias = jnp.pad(b_qv[:, 0], ((0, 0), (0, 1), (0, 0)))
    head_bias = jnp.where(first, head_bias[:, :3], head_bias[:, 3:])
    head_bias = jnp.concatenate(
        [head_bias[..., :HD], jnp.zeros_like(head_bias[..., :HD]), head_bias[..., HD:]], axis=-1
    ).reshape(LAYERS, 3 * QW)
    fc_bias = jnp.concatenate([b_fc, swap_x(b_fc, 2)], axis=1)

    vectors = widen(
        jnp.concatenate([ln_gain.reshape(4, D), ln_bias.reshape(4, D), b_out, b_down], axis=0)
    )
    gains = vectors[0:4].reshape(LAYERS, 2, DP)
    shifts = vectors[4:8].reshape(LAYERS, 2, DP)
    out_bias, down_bias = vectors[8:10], vectors[10:12]

    hidden = widen(tokens[0])
    gradient = widen(cotangent[0])
    stored = []
    for l in range(LAYERS):
        w_heads, w_hidden = weights[l]
        normed, xhat, rstd = norm_forward(hidden, gains[l, 0], shifts[l, 0], mask)
        normed_all = gather_rows(normed)
        if l == 0:
            normed_all, w_fc_b, w_down_b = lax.optimization_barrier(
                (normed_all, w_fc[1], w_down[1])
            )
            weights[1] = (weights[1][0], fetch(exchanged_hidden(w_fc_b, w_down_b)))
        qkv = project(normed_all, w_heads, 0, 3 * QW, head_bias[l])
        attended, log_total = attend_forward(live, places, qkv)
        middle = hidden + (sum_rows(attended, w_heads, 3 * QW, HW) + out_bias[l])
        normed_two, xhat_two, rstd_two = norm_forward(middle, gains[l, 1], shifts[l, 1], mask)
        normed_two_all = gather_pair(normed_two)
        inner = dot(normed_two_all, w_hidden[:, :FC], ((1,), (0,))) + fc_bias[l]
        activated = gelu_exact(inner).astype(BF)
        down_out = dot(activated, w_hidden[:, FC:], ((1,), (1,)))
        hidden = middle + (sum_pair(down_out) + down_bias[l])
        stored.append(
            (
                normed_all,
                xhat,
                rstd,
                qkv,
                log_total,
                attended,
                normed_two_all,
                xhat_two,
                rstd_two,
                inner,
                activated,
            )
        )
    mixed = narrow(hidden.astype(BF)).astype(BF)

    small = [None] * LAYERS
    fc_biases, head_biases = [], []
    high = tp // 2 == 1
    hidden_sums = [None] * LAYERS

    def own_hidden(v):
        mine = jnp.where(first, v[:WIDE], v[WIDE:])
        theirs = jnp.where(first, v[WIDE:], v[:WIDE])

        def piece(rows, h):
            return jnp.concatenate(
                [rows[:, h * FR : (h + 1) * FR], rows[:, FC + h * FR : FC + (h + 1) * FR]], axis=1
            )

        came = [swap_x(piece(theirs if m % 2 else mine, m // 2), m).astype(F32) for m in (1, 2, 3)]
        return ((piece(mine, 0).astype(F32) + came[0]) + (came[1] + came[2]))[:CHUNK]

    def to_owner(v, dim):
        v = v.reshape((1,) * dim + v.shape)
        v = lax.psum_scatter(v, "shard", scatter_dimension=dim, tiled=True)
        return lax.optimization_barrier(v).reshape(v.shape[-2:])

    for l in reversed(range(LAYERS)):
        w_heads, w_hidden = weights[l]
        (
            normed_all,
            xhat,
            rstd,
            qkv,
            log_total,
            attended,
            normed_two_all,
            xhat_two,
            rstd_two,
            inner,
            activated,
        ) = stored[l]
        g_low = gradient.astype(BF)
        g_all = gather_pair(g_low)
        grad_down_b = jnp.sum(g_low.astype(F32), axis=0)
        grad_activated = dot(g_all, w_hidden[:, FC:], ((1,), (0,)))
        grad_inner = jax.vjp(gelu_exact, inner)[1](grad_activated)[0].astype(BF)
        grad_fc_b = jnp.sum(grad_inner.astype(F32), axis=0)
        hidden_sums[l] = to_owner(
            hidden_grads(
                normed_two_all, grad_inner, g_all, activated, head_grads if l == 0 else None
            ),
            1 - l,
        )
        grad_two = sum_pair(dot(grad_inner, w_hidden[:, :FC], ((1,), (1,))))
        dx, gain_two, shift_two = norm_backward(grad_two, xhat_two, rstd_two, gains[l, 1], mask)
        grad_middle = gradient + dx
        m_low = grad_middle.astype(BF)
        m_all = gather_rows(m_low)
        grad_out_b = jnp.sum(m_low.astype(F32), axis=0)
        grad_heads = project(m_all, w_heads, 3 * QW, HW, jnp.zeros((QW,), F32))
        grad_qkv = attend_backward(live, places, log_total, grad_heads, qkv)
        if l == 0:
            hidden_own = [None, own_hidden(hidden_sums[1])]
            grad_qkv, hidden_own[1] = lax.optimization_barrier((grad_qkv, hidden_own[1]))
        head_grads = head_grads_of(normed_all, grad_qkv, m_all, attended)
        qkv_b = jnp.sum(grad_qkv.astype(F32), axis=0)
        grad_one = sum_rows(grad_qkv, w_heads, 0, 3 * QW)
        dx, gain_one, shift_one = norm_backward(grad_one, xhat, rstd, gains[l, 0], mask)
        gradient = grad_middle + dx
        small[l] = [gain_one, gain_two, shift_one, shift_two, grad_out_b, grad_down_b]
        fc_biases.append(
            jnp.where(high, jnp.roll(grad_fc_b, FR), grad_fc_b)
        )
        head_biases.append(qkv_b)

    line = sum_line_parts(
        jnp.stack(small[0] + small[1]),
        jnp.pad(jnp.stack(fc_biases[::-1]), ((0, 0), (0, 2 * DP - FC))).reshape(4, DP),
    )
    head_sum_a = to_shards(head_grads)
    line, head_sum_a, hidden_sums[0] = lax.optimization_barrier(
        (line, head_sum_a, hidden_sums[0])
    )
    own = jnp.pad(jnp.stack(head_biases[::-1]), ((0, 0), (0, DP - 3 * QW)))
    other = swap_ctx(own)
    both = jnp.concatenate([jnp.where(first, own, other), jnp.where(first, other, own)], axis=0)
    sums = sum_shards(jnp.concatenate([line, both], axis=0))
    vectors = narrow(sums[:12]).reshape(LAYERS, 6, D)
    fc_sum = sums[12:16].reshape(LAYERS, 2 * DP)
    fc_sum = jnp.where(high, fc_sum[:, FR : 2 * FR], fc_sum[:, :FR])
    halves = sums[16:].reshape(2, LAYERS, DP)[:, :, : 3 * QW].reshape(2, LAYERS, 3, 3, HD)
    head_sum = jnp.concatenate([halves[0], halves[1, :, :2]], axis=1)
    head_sum = jnp.concatenate([head_sum[:, :, 0], head_sum[:, :, 2]], axis=-1)

    def own_features(v):
        keep = jnp.where(first, v[:WIDE], v[WIDE:])
        recv = swap_ctx(jnp.where(first, v[WIDE:], v[:WIDE]))
        return (
            jnp.where(first, keep, recv)[:CHUNK].astype(F32),
            jnp.where(first, recv, keep)[:CHUNK].astype(F32),
        )

    head_sums = [jnp.sum(head_sum_a.astype(F32), axis=0).astype(BF), hidden_sums[0][:, 2 * FC :]]
    hidden_own[0] = own_hidden(hidden_sums[0][:, : 2 * FC])
    grads = [[], [], [], []]
    for l in range(LAYERS):
        a, b = own_features(head_sums[l])
        qkv = jnp.concatenate([a[:, : 3 * QW], b[:, : 2 * QW]], axis=1).reshape(CHUNK, 5, 3 * HD)
        grads[0].append(jnp.moveaxis(qkv, 1, 0))
        outs = jnp.concatenate([a[:, 3 * QW :], b[:, 3 * QW : 3 * QW + 2 * HD]], axis=1)
        grads[1].append(outs.T.reshape(5, HD, CHUNK))
        both = hidden_own[l]
        grads[2].append(both[:, :FR])
        grads[3].append(both[:, FR:].T)

    return (
        mixed[None],
        narrow(gradient)[None],
        vectors[:, 0:2],
        vectors[:, 2:4],
        jnp.stack(grads[0])[:, None],
        head_sum[:, None],
        jnp.stack(grads[1])[:, None],
        vectors[:, 4],
        jnp.stack(grads[2]),
        fc_sum,
        jnp.stack(grads[3]),
        vectors[:, 5],
    )


def solution(mesh):
    in_specs = (
        P("shard", ("ctx", "tp"), None),
        P("shard", ("ctx", "tp"), None),
        P(),
        P(),
        P(),
        P(),
        P(None, "tp", None, ("shard", "ctx"), None),
        P(None, "tp", None, None),
        P(None, "tp", None, None, ("shard", "ctx")),
        P(),
        P(None, ("shard", "ctx"), "tp"),
        P(None, "tp"),
        P(None, "tp", ("shard", "ctx")),
        P(),
    )
    out_specs = (
        P("shard", ("ctx", "tp"), None),
        P("shard", ("ctx", "tp"), None),
        P(),
        P(),
        P(None, "tp", None, ("shard", "ctx"), None),
        P(None, "tp", None, None),
        P(None, "tp", None, None, ("shard", "ctx")),
        P(),
        P(None, ("shard", "ctx"), "tp"),
        P(None, "tp"),
        P(None, "tp", ("shard", "ctx")),
        P(),
    )
    return jax.shard_map(shards, mesh=mesh, in_specs=in_specs, out_specs=out_specs, check_vma=False)
```

```python
import jax
import jax.numpy as jnp
from jax import lax
from jax.experimental import pallas as pl
from jax.experimental.pallas import tpu as pltpu
from jax.sharding import PartitionSpec as P

D = 1088
HD = 64
LAYERS = 2
EPS = 1e-05
SHARDS = 16
CHUNK = 34
WIDE = 36
DP = 2 * SHARDS * WIDE
HEADS_HERE = 3
QW = HEADS_HERE * HD
FR = 1088
FC = 2 * FR
HW = 4 * QW
ROWS = 128
BF = jnp.bfloat16
F32 = jnp.float32
LINE = ("ctx", "tp")


def line_perm(target):
    pairs = []
    for c in range(2):
        for h in range(2):
            for k in range(2):
                x2, k2 = target(2 * h + c, k)
                pairs.append((c * 4 + h * 2 + k, (x2 % 2) * 4 + (x2 // 2) * 2 + k2))
    return pairs


def swap_core(v):
    return lax.ppermute(v, LINE, line_perm(lambda x, k: (x, 1 - k)))


def swap_x(v, m):
    return lax.ppermute(v, LINE, line_perm(lambda x, k: (x ^ m, k)))


def swap_ctx(v):
    return lax.ppermute(v, "ctx", [(0, 1), (1, 0)])


def swap_shard(v, m):
    return lax.ppermute(v, "shard", [(i, i ^ m) for i in range(SHARDS)])


def gather_shards(copies):
    return lax.all_to_all(copies, "shard", 0, 0, tiled=True).reshape(-1, copies.shape[2])


def to_shards(v):
    v = v.reshape(SHARDS, v.shape[0] // SHARDS, v.shape[1])
    return lax.all_to_all(v, "shard", 0, 0, tiled=True)


def gather_pair(piece):
    return jnp.concatenate([piece, swap_core(piece)], axis=0)


def sum_pair(partial):
    return partial[:ROWS] + swap_core(partial[ROWS:].astype(BF)).astype(F32)


def gather_rows(piece):
    mine = jnp.concatenate([piece] + [swap_x(piece, m) for m in (1, 2, 3)], axis=0)
    return mine, swap_core(mine)


def sum_rows(rows, w, lo, hi, beside=None, apart=False):
    arrived = swap_core(dot(rows[HALF:], w[:, lo:hi], ((1,), (1,))).astype(BF))
    own, *others = chip_sum(rows, w, arrived, lo, hi)
    parts = [swap_x(v, m) for m, v in zip((1, 2, 3), others)]
    extra = None
    if beside is not None:
        own, rows = lax.optimization_barrier((own, rows))
        extra = beside(rows)
        if not apart:
            parts, extra = lax.optimization_barrier((parts, extra))
    parts = [v.astype(F32) for v in parts]
    return (own + parts[0]) + (parts[1] + parts[2]), extra


def sum_shards(v, step):
    return (v + swap_shard(v, step)) + (swap_shard(v, 2 * step) + swap_shard(v, 3 * step))


def sum_line_parts(both_cores, each_core):
    v = jnp.concatenate([both_cores + swap_core(both_cores), each_core], axis=0)
    return (v + swap_x(v, 1)) + (swap_x(v, 2) + swap_x(v, 3))


def dot(a, b, dims):
    return lax.dot_general(a, b, (dims, ((), ())), preferred_element_type=F32)


def norm_forward(x, gain, shift, mask):
    mean = jnp.sum(x, axis=-1, keepdims=True) * (1.0 / D)
    centred = (x - mean) * mask
    var = jnp.sum(centred * centred, axis=-1, keepdims=True) * (1.0 / D)
    rstd = lax.rsqrt(var + EPS)
    xhat = centred * rstd
    return (xhat * gain + shift).astype(BF), xhat, rstd


def norm_backward(dy, xhat, rstd, gain, mask):
    e = dy * gain
    mean_e = jnp.sum(e, axis=-1, keepdims=True) * (1.0 / D)
    mean_ex = jnp.sum(e * xhat, axis=-1, keepdims=True) * (1.0 / D)
    dx = rstd * (e - mean_e - xhat * mean_ex) * mask
    return dx, jnp.sum(dy * xhat, axis=0), jnp.sum(dy, axis=0)


def normal_cdf(v):
    return 0.5 + 0.5 * lax.erf(v * 0.5**0.5)


def gelu_slope(v):
    return normal_cdf(v) + v * jnp.exp(-0.5 * v * v) * (2 * jnp.pi) ** -0.5


LINE_ROWS = 8 * ROWS
Q_ROWS = 256
PLAIN = (((1,), (0,)), ((), ()))
TURN_RIGHT = (((1,), (1,)), ((), ()))
TURN_LEFT = (((0,), (0,)), ((), ()))


def mul(a, b, dims):
    return lax.dot_general(a, b, dims, preferred_element_type=F32)


def head_parts(ref, rows, j):
    at = 3 * HD * j
    return [ref[rows, at + i * HD : at + (i + 1) * HD] for i in range(3)]


def attend_body(live_ref, kp_ref, qp_ref, qkv_ref, out_ref, lse_ref):
    mine = pl.ds(pl.multiple_of(pl.program_id(0) * Q_ROWS, Q_ROWS), Q_ROWS)
    allowed = kp_ref[...] <= qp_ref[...]
    for j in range(HEADS_HERE):
        queries = qkv_ref[mine, 3 * HD * j : 3 * HD * j + HD]
        _, keys, values = head_parts(qkv_ref, slice(None), j)
        scores = jnp.where(allowed, mul(keys, queries, TURN_RIGHT) * HD**-0.5, -1e30)
        highest = jnp.max(scores, axis=0, keepdims=True)
        exponent = jnp.exp(scores - highest)
        totals = jnp.sum(exponent, axis=0, keepdims=True)
        probs = (exponent * (1.0 / totals)).astype(BF)
        heads = mul(values, probs, TURN_LEFT) * live_ref[j]
        out_ref[:, j * HD : (j + 1) * HD] = heads.T.astype(BF)
        lse_ref[j : j + 1, :] = highest + jnp.log(totals)
    lse_ref[HEADS_HERE:, :] = jnp.zeros((8 - HEADS_HERE, Q_ROWS), F32)


def attend_back_body(
    live_ref, kp_ref, qp_ref, lse_ref, dout_ref, qkv_ref, out_ref, key_sum, value_sum
):
    step = pl.program_id(0)
    mine = pl.ds(pl.multiple_of(step * Q_ROWS, Q_ROWS), Q_ROWS)
    allowed = kp_ref[...] <= qp_ref[...]

    @pl.when(step == 0)
    def _():
        key_sum[...] = jnp.zeros_like(key_sum)
        value_sum[...] = jnp.zeros_like(value_sum)

    for j in range(HEADS_HERE):
        queries = qkv_ref[mine, 3 * HD * j : 3 * HD * j + HD]
        _, keys, values = head_parts(qkv_ref, slice(None), j)
        dout = dout_ref[:, j * HD : (j + 1) * HD] * live_ref[j].astype(BF)
        scores = jnp.where(allowed, mul(keys, queries, TURN_RIGHT) * HD**-0.5, -1e30)
        probs = jnp.exp(scores - lse_ref[j : j + 1, :])
        dprobs = mul(values, dout, TURN_RIGHT)
        dscores = probs * (dprobs - jnp.sum(dprobs * probs, axis=0, keepdims=True))
        dscores = dscores.astype(BF)
        value_sum[j] += mul(probs.astype(BF), dout, PLAIN)
        key_sum[j] += mul(dscores, queries, PLAIN)
        dqueries = mul(keys, dscores, TURN_LEFT) * HD**-0.5
        out_ref[mine, 3 * HD * j : 3 * HD * j + HD] = dqueries.T.astype(BF)

    @pl.when(step == LINE_ROWS // Q_ROWS - 1)
    def _():
        for j in range(HEADS_HERE):
            at = 3 * HD * j
            out_ref[:, at + HD : at + 2 * HD] = (key_sum[j] * HD**-0.5).astype(BF)
            out_ref[:, at + 2 * HD : at + 3 * HD] = value_sum[j].astype(BF)


def attend_specs():
    return [
        pl.BlockSpec(memory_space=pltpu.SMEM),
        pl.BlockSpec((LINE_ROWS, 1), lambda i: (0, 0)),
        pl.BlockSpec((1, Q_ROWS), lambda i: (0, i)),
    ]


def attend_forward(live, places, qkv):
    return pl.pallas_call(
        attend_body,
        grid=(LINE_ROWS // Q_ROWS,),
        in_specs=attend_specs() + [pl.BlockSpec((LINE_ROWS, 3 * QW), lambda i: (0, 0))],
        out_specs=[
            pl.BlockSpec((Q_ROWS, QW), lambda i: (i, 0)),
            pl.BlockSpec((8, Q_ROWS), lambda i: (0, i)),
        ],
        out_shape=[
            jax.ShapeDtypeStruct((LINE_ROWS, QW), BF),
            jax.ShapeDtypeStruct((8, LINE_ROWS), F32),
        ],
        compiler_params=pltpu.CompilerParams(vmem_limit_bytes=48 << 20),
        cost_estimate=pl.CostEstimate(
            flops=4 * HEADS_HERE * LINE_ROWS * LINE_ROWS * HD * 4,
            bytes_accessed=LINE_ROWS * 4 * QW * 2,
            transcendentals=HEADS_HERE * LINE_ROWS * LINE_ROWS,
        ),
        name="attend",
    )(live, places[:, None], places[None, :], qkv)


def attend_backward(live, places, lse, dout, qkv):
    return pl.pallas_call(
        attend_back_body,
        grid=(LINE_ROWS // Q_ROWS,),
        in_specs=attend_specs()
        + [
            pl.BlockSpec((8, Q_ROWS), lambda i: (0, i)),
            pl.BlockSpec((Q_ROWS, QW), lambda i: (i, 0)),
            pl.BlockSpec((LINE_ROWS, 3 * QW), lambda i: (0, 0)),
        ],
        out_specs=pl.BlockSpec((LINE_ROWS, 3 * QW), lambda i: (0, 0)),
        out_shape=jax.ShapeDtypeStruct((LINE_ROWS, 3 * QW), BF),
        scratch_shapes=[pltpu.VMEM((HEADS_HERE, LINE_ROWS, HD), F32)] * 2,
        compiler_params=pltpu.CompilerParams(vmem_limit_bytes=48 << 20),
        cost_estimate=pl.CostEstimate(
            flops=10 * HEADS_HERE * LINE_ROWS * LINE_ROWS * HD * 4,
            bytes_accessed=LINE_ROWS * 7 * QW * 2,
            transcendentals=HEADS_HERE * LINE_ROWS * LINE_ROWS,
        ),
        name="attend_back",
    )(live, places[:, None], places[None, :], lse, dout, qkv)


def head_halves(w_qkv, w_out):
    cols = jnp.moveaxis(w_qkv, 0, 1).reshape(CHUNK, 15 * HD)
    outs = w_out.reshape(5 * HD, CHUNK).T
    gap = ((0, 0), (0, HD))
    return (
        jnp.concatenate([cols[:, : 3 * QW], outs[:, :QW]], axis=1),
        jnp.concatenate(
            [jnp.pad(cols[:, 3 * QW :], ((0, 0), (0, QW))), jnp.pad(outs[:, QW:], gap)], axis=1
        ),
    )


HALF = 4 * ROWS
GRAD_ROWS = 384


def project(pair, w, lo, hi, bias):
    def body(mine, other, w_ref, bias_ref, out_ref):
        for at, x in ((0, mine), (HALF, other)):
            got = mul(x[...], w_ref[:, lo:hi], PLAIN) + bias_ref[...]
            out_ref[at : at + HALF, :] = got.astype(BF)

    half = pl.BlockSpec((HALF, DP), lambda i: (0, 0))
    return pl.pallas_call(
        body,
        grid=(1,),
        in_specs=[
            half,
            half,
            pl.BlockSpec((DP, HW), lambda i: (0, 0)),
            pl.BlockSpec((1, hi - lo), lambda i: (0, 0)),
        ],
        out_specs=pl.BlockSpec((2 * HALF, hi - lo), lambda i: (0, 0)),
        out_shape=jax.ShapeDtypeStruct((2 * HALF, hi - lo), BF),
        compiler_params=pltpu.CompilerParams(vmem_limit_bytes=48 << 20),
        cost_estimate=pl.CostEstimate(
            flops=4 * HALF * DP * (hi - lo), bytes_accessed=8 << 20, transcendentals=0
        ),
        name="project",
    )(*pair, w, bias.reshape(1, hi - lo))


def chip_sum(rows, w, arrived, lo, hi):
    def body(rows_ref, w_ref, arrived_ref, *outs):
        w_part = w_ref[:, lo:hi]
        for m, out in enumerate(outs):
            block = slice(m * ROWS, (m + 1) * ROWS)
            got = mul(rows_ref[block, :], w_part, TURN_RIGHT) + arrived_ref[block, :].astype(F32)
            out[...] = got.astype(out.dtype)

    return pl.pallas_call(
        body,
        grid=(1,),
        in_specs=[
            pl.BlockSpec((HALF, hi - lo), lambda i: (0, 0)),
            pl.BlockSpec((DP, HW), lambda i: (0, 0)),
            pl.BlockSpec((HALF, DP), lambda i: (0, 0)),
        ],
        out_specs=[pl.BlockSpec((ROWS, DP), lambda i: (0, 0))] * 4,
        out_shape=[jax.ShapeDtypeStruct((ROWS, DP), F32 if m == 0 else BF) for m in range(4)],
        compiler_params=pltpu.CompilerParams(vmem_limit_bytes=48 << 20),
        cost_estimate=pl.CostEstimate(
            flops=2 * HALF * DP * (hi - lo), bytes_accessed=6 << 20, transcendentals=0
        ),
        name="chip_sum",
    )(rows, w, arrived)


def head_grads_of(pair, dqkv, m_pair, attended):
    def body(x0, x1, m0, m1, dqkv_ref, att_ref, out_ref):
        got = mul(x0[...], dqkv_ref[:HALF, :], TURN_LEFT)
        got += mul(x1[...], dqkv_ref[HALF:, :], TURN_LEFT)
        out_ref[:, : 3 * QW] = got.astype(BF)
        got = mul(m0[...], att_ref[:HALF, :], TURN_LEFT)
        got += mul(m1[...], att_ref[HALF:, :], TURN_LEFT)
        out_ref[:, 3 * QW :] = got.astype(BF)

    feature = pl.BlockSpec((HALF, GRAD_ROWS), lambda i: (0, i))
    return pl.pallas_call(
        body,
        grid=(DP // GRAD_ROWS,),
        in_specs=[feature] * 4
        + [
            pl.BlockSpec((2 * HALF, 3 * QW), lambda i: (0, 0)),
            pl.BlockSpec((2 * HALF, QW), lambda i: (0, 0)),
        ],
        out_specs=pl.BlockSpec((GRAD_ROWS, HW), lambda i: (i, 0)),
        out_shape=jax.ShapeDtypeStruct((DP, HW), BF),
        compiler_params=pltpu.CompilerParams(vmem_limit_bytes=48 << 20),
        cost_estimate=pl.CostEstimate(
            flops=4 * HALF * DP * HW, bytes_accessed=8 << 20, transcendentals=0
        ),
        name="head_grads",
    )(*pair, *m_pair, dqkv, attended)


def hidden_grads_body(heads, x_ref, dinner_ref, g_ref, act_ref, *refs):
    out_ref = refs[-1]
    turned = (((0,), (0,)), ((), ()))
    out_ref[:, :FC] = lax.dot_general(
        x_ref[...], dinner_ref[...], turned, preferred_element_type=F32
    ).astype(BF)
    out_ref[:, FC : 2 * FC] = lax.dot_general(
        g_ref[...], act_ref[...], turned, preferred_element_type=F32
    ).astype(BF)
    if heads:
        out_ref[:, 2 * FC :] = refs[0][...]


def hidden_grads(x, dinner, g, act, head_grads=None):
    rows = x.shape[0]
    wide = 2 * FC + (0 if head_grads is None else HW)
    args = [x, dinner, g, act] + ([] if head_grads is None else [head_grads])
    feature = pl.BlockSpec((rows, GRAD_ROWS), lambda i: (0, i))
    whole = pl.BlockSpec((rows, FC), lambda i: (0, 0))
    specs = [feature, whole, feature, whole]
    if head_grads is not None:
        specs.append(pl.BlockSpec((GRAD_ROWS, HW), lambda i: (i, 0)))
    return pl.pallas_call(
        lambda *refs: hidden_grads_body(head_grads is not None, *refs),
        grid=(DP // GRAD_ROWS,),
        in_specs=specs,
        out_specs=pl.BlockSpec((GRAD_ROWS, wide), lambda i: (i, 0)),
        out_shape=jax.ShapeDtypeStruct((DP, wide), BF),
        compiler_params=pltpu.CompilerParams(vmem_limit_bytes=48 << 20),
        cost_estimate=pl.CostEstimate(
            flops=4 * rows * DP * FC, bytes_accessed=2 * DP * wide, transcendentals=0
        ),
        name="hidden_grads",
    )(*args)


def shards(
    tokens,
    cotangent,
    block_order,
    head_count,
    ln_gain,
    ln_bias,
    w_qkv,
    b_qv,
    w_out,
    b_out,
    w_fc,
    b_fc,
    w_down,
    b_down,
):
    ctx = lax.axis_index("ctx")
    tp = lax.axis_index("tp")
    first = ctx == 0

    wide = jnp.arange(DP, dtype=jnp.int32)
    inside = wide % WIDE
    source = jnp.where(inside < CHUNK, wide // WIDE * CHUNK + inside, -1)
    spread = (source[None, :] == jnp.arange(D, dtype=jnp.int32)[:, None]).astype(BF)
    mask = (inside < CHUNK).astype(F32)[None, :]

    def widen(v):
        full = v.reshape(-1, D)
        out = lax.dot_general(
            full,
            spread.astype(full.dtype),
            (((1,), (0,)), ((), ())),
            precision=lax.Precision.HIGHEST if full.dtype == F32 else None,
            preferred_element_type=F32,
        )
        return out.reshape(*v.shape[:-1], DP)

    def narrow(v):
        return lax.dot_general(
            v,
            spread.astype(v.dtype),
            (((1,), (1,)), ((), ())),
            precision=lax.Precision.HIGHEST if v.dtype == F32 else None,
            preferred_element_type=F32,
        )

    def exchanged(halves):
        keep = jnp.where(first, halves[0], halves[1])
        send = jnp.where(first, halves[1], halves[0])
        recv = swap_ctx(send)
        top = jnp.where(first, keep, recv)
        low = jnp.where(first, recv, keep)
        gap = ((0, WIDE - CHUNK), (0, 0))
        return jnp.concatenate([jnp.pad(top, gap), jnp.pad(low, gap)], axis=0)

    def exchanged_hidden(w_fc, w_down):
        raw = jnp.concatenate([w_fc, w_down], axis=1)
        raw = jnp.pad(raw, ((0, WIDE - CHUNK), (0, 0)))
        p = [raw] + [swap_x(raw, m) for m in (1, 2, 3)]
        own, other = [
            jnp.concatenate([jnp.where(first, a, b), jnp.where(first, b, a)], axis=0)
            for a, b in ((p[0], p[1]), (p[2], p[3]))
        ]
        return jnp.concatenate([own[:, :FR], other[:, :FR], own[:, FR:], other[:, FR:]], axis=1)

    def fetch(pack):
        return lax.all_gather(pack, "shard", axis=0, tiled=True)

    w_fc_a, w_down_a, w_qkv_a, w_out_a = lax.optimization_barrier(
        (w_fc[0], w_down[0].T, w_qkv[0, 0], w_out[0, 0])
    )
    pack_a = exchanged(head_halves(w_qkv_a, w_out_a))
    w_qkv_b, w_out_b, pack_a = lax.optimization_barrier((w_qkv[1, 0], w_out[1, 0], pack_a))
    hidden_a = exchanged_hidden(w_fc_a, w_down_a)
    heads_b = exchanged(head_halves(w_qkv_b, w_out_b))
    copies = jnp.broadcast_to(pack_a, (SHARDS, *pack_a.shape))
    fetched_a = fetch(jnp.concatenate([heads_b, hidden_a], axis=1))
    weights = [
        (None, fetched_a[:, HW : HW + FC], fetched_a[:, HW + FC :]),
        (fetched_a, None, None),
    ]

    core = tp % 2
    x = (tp // 2) * 2 + ctx
    units = []
    for j in range(2):
        for m in range(4):
            chip = x ^ m
            block = (chip % 2) * 2 + chip // 2
            start = jnp.sum(jnp.where(jnp.arange(4) == block, block_order, 0)) * 256
            units.append(start + (core ^ j) * ROWS + jnp.arange(ROWS, dtype=jnp.int32))
    places = jnp.concatenate(units)
    my_count = jnp.sum(jnp.where(jnp.arange(4) == tp, head_count, 0))
    slot = jnp.arange(HEADS_HERE, dtype=jnp.int32) + ctx * HEADS_HERE
    live = ((slot < my_count) & (slot < 5)).astype(F32)

    head_bias = jnp.pad(b_qv[:, 0], ((0, 0), (0, 1), (0, 0)))
    head_bias = jnp.where(first, head_bias[:, :3], head_bias[:, 3:])
    head_bias = jnp.concatenate(
        [head_bias[..., :HD], jnp.zeros_like(head_bias[..., :HD]), head_bias[..., HD:]], axis=-1
    ).reshape(LAYERS, 3 * QW)
    fc_bias = jnp.concatenate([b_fc, swap_x(b_fc, 2)], axis=1)

    vectors = widen(
        jnp.concatenate([ln_gain.reshape(4, D), ln_bias.reshape(4, D), b_out, b_down], axis=0)
    )
    gains = vectors[0:4].reshape(LAYERS, 2, DP)
    shifts = vectors[4:8].reshape(LAYERS, 2, DP)
    out_bias, down_bias = vectors[8:10], vectors[10:12]

    hidden = widen(tokens[0])
    gradient = widen(cotangent[0])
    stored = []
    for l in range(LAYERS):
        w_heads = weights[l][0]
        normed, xhat, rstd = norm_forward(hidden, gains[l, 0], shifts[l, 0], mask)
        if l == 0:
            normed, copies = lax.optimization_barrier((normed, copies))
            w_heads, w_fc_b, w_down_b = lax.optimization_barrier(
                (gather_shards(copies), w_fc[1], w_down[1].T)
            )
            hidden_b = exchanged_hidden(w_fc_b, w_down_b)
            weights[0] = (w_heads, *weights[0][1:])
        normed_all = gather_rows(normed)
        qkv = project(normed_all, w_heads, 0, 3 * QW, head_bias[l])
        attended, log_total = attend_forward(live, places, qkv)
        if l == 0:
            attended, hidden_b = lax.optimization_barrier((attended, hidden_b))
            fetched_b = fetch(hidden_b)
            weights[1] = (fetched_a, fetched_b[:, :FC], fetched_b[:, FC:])
        summed, _ = sum_rows(attended, w_heads, 3 * QW, HW)
        middle = hidden + (summed + out_bias[l])
        normed_two, xhat_two, rstd_two = norm_forward(middle, gains[l, 1], shifts[l, 1], mask)
        normed_two_all = gather_pair(normed_two)
        _, w_up, w_back = weights[l]
        inner = dot(normed_two_all, w_up, ((1,), (0,))) + fc_bias[l]
        activated = (inner * normal_cdf(inner)).astype(BF)
        down_out = dot(activated, w_back, ((1,), (1,)))
        hidden = middle + (sum_pair(down_out) + down_bias[l])
        stored.append(
            (
                normed_all,
                xhat,
                rstd,
                qkv,
                log_total,
                attended,
                normed_two_all,
                xhat_two,
                rstd_two,
                inner,
                activated,
            )
        )
    mixed = narrow(hidden.astype(BF)).astype(BF)

    small = [None] * LAYERS
    fc_biases, head_biases = [], []
    high = tp // 2 == 1
    hidden_sums = [None] * LAYERS

    def own_hidden(v):
        mine = jnp.where(first, v[:WIDE], v[WIDE:])
        theirs = jnp.where(first, v[WIDE:], v[:WIDE])

        def piece(rows, h):
            return jnp.concatenate(
                [rows[:, h * FR : (h + 1) * FR], rows[:, FC + h * FR : FC + (h + 1) * FR]], axis=1
            )

        came = [swap_x(piece(theirs if m % 2 else mine, m // 2), m).astype(F32) for m in (1, 2, 3)]
        return ((piece(mine, 0).astype(F32) + came[0]) + (came[1] + came[2]))[:CHUNK]

    def to_owner(v, dim):
        v = v.reshape((1,) * dim + v.shape)
        v = lax.psum_scatter(v, "shard", scatter_dimension=dim, tiled=True)
        return lax.optimization_barrier(v).reshape(v.shape[-2:])

    for l in reversed(range(LAYERS)):
        w_heads, w_up, w_back = weights[l]
        (
            normed_all,
            xhat,
            rstd,
            qkv,
            log_total,
            attended,
            normed_two_all,
            xhat_two,
            rstd_two,
            inner,
            activated,
        ) = stored[l]
        g_low = gradient.astype(BF)
        g_all = gather_pair(g_low)
        grad_down_b = jnp.sum(g_low.astype(F32), axis=0)
        grad_activated = dot(g_all, w_back, ((1,), (0,)))
        grad_inner = (grad_activated * gelu_slope(inner)).astype(BF)
        grad_fc_b = jnp.sum(grad_inner.astype(F32), axis=0)
        hidden_sums[l] = to_owner(
            hidden_grads(
                normed_two_all, grad_inner, g_all, activated, head_grads if l == 0 else None
            ),
            1 - l,
        )
        grad_two = sum_pair(dot(grad_inner, w_up, ((1,), (1,))))
        dx, gain_two, shift_two = norm_backward(grad_two, xhat_two, rstd_two, gains[l, 1], mask)
        grad_middle = gradient + dx
        m_low = grad_middle.astype(BF)
        m_all = gather_rows(m_low)
        grad_out_b = jnp.sum(m_low.astype(F32), axis=0)
        grad_heads = project(m_all, w_heads, 3 * QW, HW, jnp.zeros((QW,), F32))
        grad_qkv = attend_backward(live, places, log_total, grad_heads, qkv)
        if l == 0:
            hidden_own = [None, own_hidden(hidden_sums[1])]
            grad_qkv, hidden_own[1] = lax.optimization_barrier((grad_qkv, hidden_own[1]))
        qkv_b = jnp.sum(grad_qkv.astype(F32), axis=0)
        grad_one, head_grads = sum_rows(
            grad_qkv,
            w_heads,
            0,
            3 * QW,
            lambda rows: head_grads_of(normed_all, rows, m_all, attended),
            apart=l == 0,
        )
        dx, gain_one, shift_one = norm_backward(grad_one, xhat, rstd, gains[l, 0], mask)
        gradient = grad_middle + dx
        small[l] = [gain_one, gain_two, shift_one, shift_two, grad_out_b, grad_down_b]
        fc_biases.append(
            jnp.where(high, jnp.roll(grad_fc_b, FR), grad_fc_b)
        )
        head_biases.append(qkv_b)

    head_sum_a = to_shards(head_grads)

    line = sum_line_parts(
        jnp.stack(small[0] + small[1]),
        jnp.pad(jnp.stack(fc_biases[::-1]), ((0, 0), (0, 2 * DP - FC))).reshape(4, DP),
    )
    own = jnp.pad(jnp.stack(head_biases[::-1]), ((0, 0), (0, DP - 3 * QW)))
    other = swap_ctx(own)
    both = jnp.concatenate([jnp.where(first, own, other), jnp.where(first, other, own)], axis=0)
    sums = sum_shards(jnp.concatenate([line, both], axis=0), 1)
    sums, head_sum_a, hidden_sums[0] = lax.optimization_barrier(
        (sums, head_sum_a, hidden_sums[0])
    )
    sums = sum_shards(sums, 4)
    vectors = narrow(sums[:12]).reshape(LAYERS, 6, D)
    fc_sum = sums[12:16].reshape(LAYERS, 2 * DP)
    fc_sum = jnp.where(high, fc_sum[:, FR : 2 * FR], fc_sum[:, :FR])
    halves = sums[16:].reshape(2, LAYERS, DP)[:, :, : 3 * QW].reshape(2, LAYERS, 3, 3, HD)
    head_sum = jnp.concatenate([halves[0], halves[1, :, :2]], axis=1)
    head_sum = jnp.concatenate([head_sum[:, :, 0], head_sum[:, :, 2]], axis=-1)

    def own_features(v):
        keep = jnp.where(first, v[:WIDE], v[WIDE:])
        recv = swap_ctx(jnp.where(first, v[WIDE:], v[:WIDE]))
        return (
            jnp.where(first, keep, recv)[:CHUNK].astype(F32),
            jnp.where(first, recv, keep)[:CHUNK].astype(F32),
        )

    head_sums = [jnp.sum(head_sum_a.astype(F32), axis=0).astype(BF), hidden_sums[0][:, 2 * FC :]]
    hidden_own[0] = own_hidden(hidden_sums[0][:, : 2 * FC])
    grads = [[], [], [], []]
    for l in range(LAYERS):
        a, b = own_features(head_sums[l])
        qkv = jnp.concatenate([a[:, : 3 * QW], b[:, : 2 * QW]], axis=1).reshape(CHUNK, 5, 3 * HD)
        grads[0].append(jnp.moveaxis(qkv, 1, 0))
        outs = jnp.concatenate([a[:, 3 * QW :], b[:, 3 * QW : 3 * QW + 2 * HD]], axis=1)
        grads[1].append(outs.T.reshape(5, HD, CHUNK))
        both = hidden_own[l]
        grads[2].append(both[:, :FR])
        grads[3].append(both[:, FR:].T)

    return (
        mixed[None],
        narrow(gradient)[None],
        vectors[:, 0:2],
        vectors[:, 2:4],
        jnp.stack(grads[0])[:, None],
        head_sum[:, None],
        jnp.stack(grads[1])[:, None],
        vectors[:, 4],
        jnp.stack(grads[2]),
        fc_sum,
        jnp.stack(grads[3]),
        vectors[:, 5],
    )


def solution(mesh):
    in_specs = (
        P("shard", ("ctx", "tp"), None),
        P("shard", ("ctx", "tp"), None),
        P(),
        P(),
        P(),
        P(),
        P(None, "tp", None, ("shard", "ctx"), None),
        P(None, "tp", None, None),
        P(None, "tp", None, None, ("shard", "ctx")),
        P(),
        P(None, ("shard", "ctx"), "tp"),
        P(None, "tp"),
        P(None, "tp", ("shard", "ctx")),
        P(),
    )
    out_specs = (
        P("shard", ("ctx", "tp"), None),
        P("shard", ("ctx", "tp"), None),
        P(),
        P(),
        P(None, "tp", None, ("shard", "ctx"), None),
        P(None, "tp", None, None),
        P(None, "tp", None, None, ("shard", "ctx")),
        P(),
        P(None, ("shard", "ctx"), "tp"),
        P(None, "tp"),
        P(None, "tp", ("shard", "ctx")),
        P(),
    )
    return jax.shard_map(shards, mesh=mesh, in_specs=in_specs, out_specs=out_specs, check_vma=False)
```

```python
import jax
import jax.numpy as jnp
from jax import lax
from jax.experimental import pallas as pl
from jax.experimental.pallas import tpu as pltpu
from jax.sharding import PartitionSpec as P

D = 1088
HD = 64
LAYERS = 2
EPS = 1e-05
SHARDS = 16
CHUNK = 34
WIDE = 36
DP = 2 * SHARDS * WIDE
HEADS_HERE = 3
QW = HEADS_HERE * HD
FR = 1088
FC = 2 * FR
HW = 4 * QW
ROWS = 128
BF = jnp.bfloat16
F32 = jnp.float32
LINE = ("ctx", "tp")


def line_perm(target):
    pairs = []
    for c in range(2):
        for h in range(2):
            for k in range(2):
                x2, k2 = target(2 * h + c, k)
                pairs.append((c * 4 + h * 2 + k, (x2 % 2) * 4 + (x2 // 2) * 2 + k2))
    return pairs


def swap_core(v):
    return lax.ppermute(v, LINE, line_perm(lambda x, k: (x, 1 - k)))


def swap_x(v, m):
    return lax.ppermute(v, LINE, line_perm(lambda x, k: (x ^ m, k)))


def swap_ctx(v):
    return lax.ppermute(v, "ctx", [(0, 1), (1, 0)])


def swap_shard(v, m):
    return lax.ppermute(v, "shard", [(i, i ^ m) for i in range(SHARDS)])


def gather_shards(copies):
    return lax.all_to_all(copies, "shard", 0, 0, tiled=True).reshape(-1, copies.shape[2])


def to_shards(v):
    v = v.reshape(SHARDS, v.shape[0] // SHARDS, v.shape[1])
    return lax.all_to_all(v, "shard", 0, 0, tiled=True)


def gather_pair(piece):
    return jnp.concatenate([piece, swap_core(piece)], axis=0)


def sum_pair(partial):
    return partial[:ROWS] + swap_core(partial[ROWS:].astype(BF)).astype(F32)


def gather_rows(piece):
    mine = jnp.concatenate([piece] + [swap_x(piece, m) for m in (1, 2, 3)], axis=0)
    return mine, swap_core(mine)


def sum_rows(rows, w, lo, hi, beside=None, apart=False):
    arrived = swap_core(dot(rows[HALF:], w[:, lo:hi], ((1,), (1,))).astype(BF))
    own, *others = chip_sum(rows, w, arrived, lo, hi)
    parts = [swap_x(v, m) for m, v in zip((1, 2, 3), others)]
    extra = None
    if beside is not None:
        own, rows = lax.optimization_barrier((own, rows))
        extra = beside(rows)
        if not apart:
            parts, extra = lax.optimization_barrier((parts, extra))
    parts = [v.astype(F32) for v in parts]
    return (own + parts[0]) + (parts[1] + parts[2]), extra


def sum_shards(v, step):
    return (v + swap_shard(v, step)) + (swap_shard(v, 2 * step) + swap_shard(v, 3 * step))


def sum_line_parts(both_cores, each_core):
    v = jnp.concatenate([both_cores + swap_core(both_cores), each_core], axis=0)
    return (v + swap_x(v, 1)) + (swap_x(v, 2) + swap_x(v, 3))


def dot(a, b, dims):
    return lax.dot_general(a, b, (dims, ((), ())), preferred_element_type=F32)


def norm_forward(x, gain, shift, mask):
    mean = jnp.sum(x, axis=-1, keepdims=True) * (1.0 / D)
    centred = (x - mean) * mask
    var = jnp.sum(centred * centred, axis=-1, keepdims=True) * (1.0 / D)
    rstd = lax.rsqrt(var + EPS)
    xhat = centred * rstd
    return (xhat * gain + shift).astype(BF), xhat, rstd


def norm_backward(dy, xhat, rstd, gain, mask):
    e = dy * gain
    mean_e = jnp.sum(e, axis=-1, keepdims=True) * (1.0 / D)
    mean_ex = jnp.sum(e * xhat, axis=-1, keepdims=True) * (1.0 / D)
    dx = rstd * (e - mean_e - xhat * mean_ex) * mask
    return dx, jnp.sum(dy * xhat, axis=0), jnp.sum(dy, axis=0)


def normal_cdf(v):
    return 0.5 + 0.5 * lax.erf(v * 0.5**0.5)


def gelu_slope(v):
    return normal_cdf(v) + v * jnp.exp(-0.5 * v * v) * (2 * jnp.pi) ** -0.5


LINE_ROWS = 8 * ROWS
Q_ROWS = 256
PLAIN = (((1,), (0,)), ((), ()))
TURN_RIGHT = (((1,), (1,)), ((), ()))
TURN_LEFT = (((0,), (0,)), ((), ()))


def mul(a, b, dims):
    return lax.dot_general(a, b, dims, preferred_element_type=F32)


def head_parts(ref, rows, j):
    at = 3 * HD * j
    return [ref[rows, at + i * HD : at + (i + 1) * HD] for i in range(3)]


def attend_body(live_ref, kp_ref, qp_ref, qkv_ref, out_ref, lse_ref):
    mine = pl.ds(pl.multiple_of(pl.program_id(0) * Q_ROWS, Q_ROWS), Q_ROWS)
    allowed = kp_ref[...] <= qp_ref[...]
    for j in range(HEADS_HERE):
        queries = qkv_ref[mine, 3 * HD * j : 3 * HD * j + HD]
        _, keys, values = head_parts(qkv_ref, slice(None), j)
        scores = jnp.where(allowed, mul(keys, queries, TURN_RIGHT) * HD**-0.5, -1e30)
        highest = jnp.max(scores, axis=0, keepdims=True)
        exponent = jnp.exp(scores - highest)
        totals = jnp.sum(exponent, axis=0, keepdims=True)
        probs = (exponent * (1.0 / totals)).astype(BF)
        heads = mul(values, probs, TURN_LEFT) * live_ref[j]
        out_ref[:, j * HD : (j + 1) * HD] = heads.T.astype(BF)
        lse_ref[j : j + 1, :] = highest + jnp.log(totals)
    lse_ref[HEADS_HERE:, :] = jnp.zeros((8 - HEADS_HERE, Q_ROWS), F32)


def attend_back_body(
    live_ref, kp_ref, qp_ref, lse_ref, dout_ref, qkv_ref, out_ref, key_sum, value_sum
):
    step = pl.program_id(0)
    mine = pl.ds(pl.multiple_of(step * Q_ROWS, Q_ROWS), Q_ROWS)
    allowed = kp_ref[...] <= qp_ref[...]

    @pl.when(step == 0)
    def _():
        key_sum[...] = jnp.zeros_like(key_sum)
        value_sum[...] = jnp.zeros_like(value_sum)

    for j in range(HEADS_HERE):
        queries = qkv_ref[mine, 3 * HD * j : 3 * HD * j + HD]
        _, keys, values = head_parts(qkv_ref, slice(None), j)
        dout = dout_ref[:, j * HD : (j + 1) * HD] * live_ref[j].astype(BF)
        scores = jnp.where(allowed, mul(keys, queries, TURN_RIGHT) * HD**-0.5, -1e30)
        probs = jnp.exp(scores - lse_ref[j : j + 1, :])
        dprobs = mul(values, dout, TURN_RIGHT)
        dscores = probs * (dprobs - jnp.sum(dprobs * probs, axis=0, keepdims=True))
        dscores = dscores.astype(BF)
        value_sum[j] += mul(probs.astype(BF), dout, PLAIN)
        key_sum[j] += mul(dscores, queries, PLAIN)
        dqueries = mul(keys, dscores, TURN_LEFT) * HD**-0.5
        out_ref[mine, 3 * HD * j : 3 * HD * j + HD] = dqueries.T.astype(BF)

    @pl.when(step == LINE_ROWS // Q_ROWS - 1)
    def _():
        for j in range(HEADS_HERE):
            at = 3 * HD * j
            out_ref[:, at + HD : at + 2 * HD] = (key_sum[j] * HD**-0.5).astype(BF)
            out_ref[:, at + 2 * HD : at + 3 * HD] = value_sum[j].astype(BF)


def attend_specs():
    return [
        pl.BlockSpec(memory_space=pltpu.SMEM),
        pl.BlockSpec((LINE_ROWS, 1), lambda i: (0, 0)),
        pl.BlockSpec((1, Q_ROWS), lambda i: (0, i)),
    ]


def attend_forward(live, places, qkv):
    return pl.pallas_call(
        attend_body,
        grid=(LINE_ROWS // Q_ROWS,),
        in_specs=attend_specs() + [pl.BlockSpec((LINE_ROWS, 3 * QW), lambda i: (0, 0))],
        out_specs=[
            pl.BlockSpec((Q_ROWS, QW), lambda i: (i, 0)),
            pl.BlockSpec((8, Q_ROWS), lambda i: (0, i)),
        ],
        out_shape=[
            jax.ShapeDtypeStruct((LINE_ROWS, QW), BF),
            jax.ShapeDtypeStruct((8, LINE_ROWS), F32),
        ],
        compiler_params=pltpu.CompilerParams(vmem_limit_bytes=48 << 20),
        cost_estimate=pl.CostEstimate(
            flops=4 * HEADS_HERE * LINE_ROWS * LINE_ROWS * HD * 4,
            bytes_accessed=LINE_ROWS * 4 * QW * 2,
            transcendentals=HEADS_HERE * LINE_ROWS * LINE_ROWS,
        ),
        name="attend",
    )(live, places[:, None], places[None, :], qkv)


def attend_backward(live, places, lse, dout, qkv):
    return pl.pallas_call(
        attend_back_body,
        grid=(LINE_ROWS // Q_ROWS,),
        in_specs=attend_specs()
        + [
            pl.BlockSpec((8, Q_ROWS), lambda i: (0, i)),
            pl.BlockSpec((Q_ROWS, QW), lambda i: (i, 0)),
            pl.BlockSpec((LINE_ROWS, 3 * QW), lambda i: (0, 0)),
        ],
        out_specs=pl.BlockSpec((LINE_ROWS, 3 * QW), lambda i: (0, 0)),
        out_shape=jax.ShapeDtypeStruct((LINE_ROWS, 3 * QW), BF),
        scratch_shapes=[pltpu.VMEM((HEADS_HERE, LINE_ROWS, HD), F32)] * 2,
        compiler_params=pltpu.CompilerParams(vmem_limit_bytes=48 << 20),
        cost_estimate=pl.CostEstimate(
            flops=10 * HEADS_HERE * LINE_ROWS * LINE_ROWS * HD * 4,
            bytes_accessed=LINE_ROWS * 7 * QW * 2,
            transcendentals=HEADS_HERE * LINE_ROWS * LINE_ROWS,
        ),
        name="attend_back",
    )(live, places[:, None], places[None, :], lse, dout, qkv)


def head_halves(w_qkv, w_out):
    cols = jnp.moveaxis(w_qkv, 0, 1).reshape(CHUNK, 15 * HD)
    outs = w_out.reshape(5 * HD, CHUNK).T
    gap = ((0, 0), (0, HD))
    return (
        jnp.concatenate([cols[:, : 3 * QW], outs[:, :QW]], axis=1),
        jnp.concatenate(
            [jnp.pad(cols[:, 3 * QW :], ((0, 0), (0, QW))), jnp.pad(outs[:, QW:], gap)], axis=1
        ),
    )


HALF = 4 * ROWS
GRAD_ROWS = 384


def project(pair, w, lo, hi, bias):
    def body(mine, other, w_ref, bias_ref, out_ref):
        for at, x in ((0, mine), (HALF, other)):
            got = mul(x[...], w_ref[:, lo:hi], PLAIN) + bias_ref[...]
            out_ref[at : at + HALF, :] = got.astype(BF)

    half = pl.BlockSpec((HALF, DP), lambda i: (0, 0))
    return pl.pallas_call(
        body,
        grid=(1,),
        in_specs=[
            half,
            half,
            pl.BlockSpec((DP, HW), lambda i: (0, 0)),
            pl.BlockSpec((1, hi - lo), lambda i: (0, 0)),
        ],
        out_specs=pl.BlockSpec((2 * HALF, hi - lo), lambda i: (0, 0)),
        out_shape=jax.ShapeDtypeStruct((2 * HALF, hi - lo), BF),
        compiler_params=pltpu.CompilerParams(vmem_limit_bytes=48 << 20),
        cost_estimate=pl.CostEstimate(
            flops=4 * HALF * DP * (hi - lo), bytes_accessed=8 << 20, transcendentals=0
        ),
        name="project",
    )(*pair, w, bias.reshape(1, hi - lo))


def chip_sum(rows, w, arrived, lo, hi):
    def body(rows_ref, w_ref, arrived_ref, *outs):
        w_part = w_ref[:, lo:hi]
        for m, out in enumerate(outs):
            block = slice(m * ROWS, (m + 1) * ROWS)
            got = mul(rows_ref[block, :], w_part, TURN_RIGHT) + arrived_ref[block, :].astype(F32)
            out[...] = got.astype(out.dtype)

    return pl.pallas_call(
        body,
        grid=(1,),
        in_specs=[
            pl.BlockSpec((HALF, hi - lo), lambda i: (0, 0)),
            pl.BlockSpec((DP, HW), lambda i: (0, 0)),
            pl.BlockSpec((HALF, DP), lambda i: (0, 0)),
        ],
        out_specs=[pl.BlockSpec((ROWS, DP), lambda i: (0, 0))] * 4,
        out_shape=[jax.ShapeDtypeStruct((ROWS, DP), F32 if m == 0 else BF) for m in range(4)],
        compiler_params=pltpu.CompilerParams(vmem_limit_bytes=48 << 20),
        cost_estimate=pl.CostEstimate(
            flops=2 * HALF * DP * (hi - lo), bytes_accessed=6 << 20, transcendentals=0
        ),
        name="chip_sum",
    )(rows, w, arrived)


def head_grads_of(pair, dqkv, m_pair, attended):
    def body(x0, x1, m0, m1, dqkv_ref, att_ref, out_ref):
        got = mul(x0[...], dqkv_ref[:HALF, :], TURN_LEFT)
        got += mul(x1[...], dqkv_ref[HALF:, :], TURN_LEFT)
        out_ref[:, : 3 * QW] = got.astype(BF)
        got = mul(m0[...], att_ref[:HALF, :], TURN_LEFT)
        got += mul(m1[...], att_ref[HALF:, :], TURN_LEFT)
        out_ref[:, 3 * QW :] = got.astype(BF)

    feature = pl.BlockSpec((HALF, GRAD_ROWS), lambda i: (0, i))
    return pl.pallas_call(
        body,
        grid=(DP // GRAD_ROWS,),
        in_specs=[feature] * 4
        + [
            pl.BlockSpec((2 * HALF, 3 * QW), lambda i: (0, 0)),
            pl.BlockSpec((2 * HALF, QW), lambda i: (0, 0)),
        ],
        out_specs=pl.BlockSpec((GRAD_ROWS, HW), lambda i: (i, 0)),
        out_shape=jax.ShapeDtypeStruct((DP, HW), BF),
        compiler_params=pltpu.CompilerParams(vmem_limit_bytes=48 << 20),
        cost_estimate=pl.CostEstimate(
            flops=4 * HALF * DP * HW, bytes_accessed=8 << 20, transcendentals=0
        ),
        name="head_grads",
    )(*pair, *m_pair, dqkv, attended)


def hidden_grads_body(heads, x_ref, dinner_ref, g_ref, act_ref, *refs):
    out_ref = refs[-1]
    turned = (((0,), (0,)), ((), ()))
    out_ref[:, :FC] = lax.dot_general(
        x_ref[...], dinner_ref[...], turned, preferred_element_type=F32
    ).astype(BF)
    out_ref[:, FC : 2 * FC] = lax.dot_general(
        g_ref[...], act_ref[...], turned, preferred_element_type=F32
    ).astype(BF)
    if heads:
        out_ref[:, 2 * FC :] = refs[0][...]


def hidden_grads(x, dinner, g, act, head_grads=None):
    rows = x.shape[0]
    wide = 2 * FC + (0 if head_grads is None else HW)
    args = [x, dinner, g, act] + ([] if head_grads is None else [head_grads])
    feature = pl.BlockSpec((rows, GRAD_ROWS), lambda i: (0, i))
    whole = pl.BlockSpec((rows, FC), lambda i: (0, 0))
    specs = [feature, whole, feature, whole]
    if head_grads is not None:
        specs.append(pl.BlockSpec((GRAD_ROWS, HW), lambda i: (i, 0)))
    return pl.pallas_call(
        lambda *refs: hidden_grads_body(head_grads is not None, *refs),
        grid=(DP // GRAD_ROWS,),
        in_specs=specs,
        out_specs=pl.BlockSpec((GRAD_ROWS, wide), lambda i: (i, 0)),
        out_shape=jax.ShapeDtypeStruct((DP, wide), BF),
        compiler_params=pltpu.CompilerParams(vmem_limit_bytes=48 << 20),
        cost_estimate=pl.CostEstimate(
            flops=4 * rows * DP * FC, bytes_accessed=2 * DP * wide, transcendentals=0
        ),
        name="hidden_grads",
    )(*args)


def shards(
    tokens,
    cotangent,
    block_order,
    head_count,
    ln_gain,
    ln_bias,
    w_qkv,
    b_qv,
    w_out,
    b_out,
    w_fc,
    b_fc,
    w_down,
    b_down,
):
    ctx = lax.axis_index("ctx")
    tp = lax.axis_index("tp")
    first = ctx == 0

    wide = jnp.arange(DP, dtype=jnp.int32)
    inside = wide % WIDE
    source = jnp.where(inside < CHUNK, wide // WIDE * CHUNK + inside, -1)
    spread = (source[None, :] == jnp.arange(D, dtype=jnp.int32)[:, None]).astype(BF)
    mask = (inside < CHUNK).astype(F32)[None, :]

    def widen(v):
        full = v.reshape(-1, D)
        out = lax.dot_general(
            full,
            spread.astype(full.dtype),
            (((1,), (0,)), ((), ())),
            precision=lax.Precision.HIGHEST if full.dtype == F32 else None,
            preferred_element_type=F32,
        )
        return out.reshape(*v.shape[:-1], DP)

    def narrow(v):
        return lax.dot_general(
            v,
            spread.astype(v.dtype),
            (((1,), (1,)), ((), ())),
            precision=lax.Precision.HIGHEST if v.dtype == F32 else None,
            preferred_element_type=F32,
        )

    def exchanged(halves):
        keep = jnp.where(first, halves[0], halves[1])
        send = jnp.where(first, halves[1], halves[0])
        recv = swap_ctx(send)
        top = jnp.where(first, keep, recv)
        low = jnp.where(first, recv, keep)
        gap = ((0, WIDE - CHUNK), (0, 0))
        return jnp.concatenate([jnp.pad(top, gap), jnp.pad(low, gap)], axis=0)

    def exchanged_hidden(w_fc, w_down):
        raw = jnp.concatenate([w_fc, w_down], axis=1)
        raw = jnp.pad(raw, ((0, WIDE - CHUNK), (0, 0)))
        p = [raw] + [swap_x(raw, m) for m in (1, 2, 3)]
        own, other = [
            jnp.concatenate([jnp.where(first, a, b), jnp.where(first, b, a)], axis=0)
            for a, b in ((p[0], p[1]), (p[2], p[3]))
        ]
        return jnp.concatenate([own[:, :FR], other[:, :FR], own[:, FR:], other[:, FR:]], axis=1)

    def fetch(pack):
        return lax.all_gather(pack, "shard", axis=0, tiled=True)

    w_fc_a, w_down_a, w_qkv_b, w_out_b = lax.optimization_barrier(
        (w_fc[0], w_down[0].T, w_qkv[1, 0], w_out[1, 0])
    )
    hidden_a = exchanged_hidden(w_fc_a, w_down_a)
    heads_b = exchanged(head_halves(w_qkv_b, w_out_b))
    joined, w_qkv_a, w_out_a = lax.optimization_barrier(
        (jnp.concatenate([heads_b, hidden_a], axis=1), w_qkv[0, 0], w_out[0, 0])
    )
    fetched_a = fetch(joined)
    pack_a = exchanged(head_halves(w_qkv_a, w_out_a))
    copies = jnp.broadcast_to(pack_a, (SHARDS, *pack_a.shape))
    weights = [
        (None, fetched_a[:, HW : HW + FC], fetched_a[:, HW + FC :]),
        (fetched_a, None, None),
    ]

    core = tp % 2
    x = (tp // 2) * 2 + ctx
    units = []
    for j in range(2):
        for m in range(4):
            chip = x ^ m
            block = (chip % 2) * 2 + chip // 2
            start = jnp.sum(jnp.where(jnp.arange(4) == block, block_order, 0)) * 256
            units.append(start + (core ^ j) * ROWS + jnp.arange(ROWS, dtype=jnp.int32))
    places = jnp.concatenate(units)
    my_count = jnp.sum(jnp.where(jnp.arange(4) == tp, head_count, 0))
    slot = jnp.arange(HEADS_HERE, dtype=jnp.int32) + ctx * HEADS_HERE
    live = ((slot < my_count) & (slot < 5)).astype(F32)

    head_bias = jnp.pad(b_qv[:, 0], ((0, 0), (0, 1), (0, 0)))
    head_bias = jnp.where(first, head_bias[:, :3], head_bias[:, 3:])
    head_bias = jnp.concatenate(
        [head_bias[..., :HD], jnp.zeros_like(head_bias[..., :HD]), head_bias[..., HD:]], axis=-1
    ).reshape(LAYERS, 3 * QW)
    fc_bias = jnp.concatenate([b_fc, swap_x(b_fc, 2)], axis=1)

    vectors = widen(
        jnp.concatenate([ln_gain.reshape(4, D), ln_bias.reshape(4, D), b_out, b_down], axis=0)
    )
    gains = vectors[0:4].reshape(LAYERS, 2, DP)
    shifts = vectors[4:8].reshape(LAYERS, 2, DP)
    out_bias, down_bias = vectors[8:10], vectors[10:12]

    hidden = widen(tokens[0])
    gradient = widen(cotangent[0])
    stored = []
    for l in range(LAYERS):
        w_heads = weights[l][0]
        normed, xhat, rstd = norm_forward(hidden, gains[l, 0], shifts[l, 0], mask)
        if l == 0:
            normed, copies = lax.optimization_barrier((normed, copies))
            w_heads, w_fc_b, w_down_b = lax.optimization_barrier(
                (gather_shards(copies), w_fc[1], w_down[1].T)
            )
            hidden_b = exchanged_hidden(w_fc_b, w_down_b)
            weights[0] = (w_heads, *weights[0][1:])
        normed_all = gather_rows(normed)
        qkv = project(normed_all, w_heads, 0, 3 * QW, head_bias[l])
        attended, log_total = attend_forward(live, places, qkv)
        if l == 0:
            attended, hidden_b = lax.optimization_barrier((attended, hidden_b))
            fetched_b = fetch(hidden_b)
            weights[1] = (fetched_a, fetched_b[:, :FC], fetched_b[:, FC:])
        summed, _ = sum_rows(attended, w_heads, 3 * QW, HW)
        middle = hidden + (summed + out_bias[l])
        normed_two, xhat_two, rstd_two = norm_forward(middle, gains[l, 1], shifts[l, 1], mask)
        normed_two_all = gather_pair(normed_two)
        _, w_up, w_back = weights[l]
        inner = dot(normed_two_all, w_up, ((1,), (0,))) + fc_bias[l]
        activated = (inner * normal_cdf(inner)).astype(BF)
        down_out = dot(activated, w_back, ((1,), (1,)))
        hidden = middle + (sum_pair(down_out) + down_bias[l])
        stored.append(
            (
                normed_all,
                xhat,
                rstd,
                qkv,
                log_total,
                attended,
                normed_two_all,
                xhat_two,
                rstd_two,
                inner,
                activated,
            )
        )
    mixed = narrow(hidden.astype(BF)).astype(BF)

    small = [None] * LAYERS
    fc_biases, head_biases = [], []
    high = tp // 2 == 1
    hidden_sums = [None] * LAYERS

    def own_hidden(v):
        mine = jnp.where(first, v[:WIDE], v[WIDE:])
        theirs = jnp.where(first, v[WIDE:], v[:WIDE])

        def piece(rows, h):
            return jnp.concatenate(
                [rows[:, h * FR : (h + 1) * FR], rows[:, FC + h * FR : FC + (h + 1) * FR]], axis=1
            )

        came = [swap_x(piece(theirs if m % 2 else mine, m // 2), m).astype(F32) for m in (1, 2, 3)]
        return ((piece(mine, 0).astype(F32) + came[0]) + (came[1] + came[2]))[:CHUNK]

    def to_owner(v, dim):
        v = v.reshape((1,) * dim + v.shape)
        v = lax.psum_scatter(v, "shard", scatter_dimension=dim, tiled=True)
        return lax.optimization_barrier(v).reshape(v.shape[-2:])

    for l in reversed(range(LAYERS)):
        w_heads, w_up, w_back = weights[l]
        (
            normed_all,
            xhat,
            rstd,
            qkv,
            log_total,
            attended,
            normed_two_all,
            xhat_two,
            rstd_two,
            inner,
            activated,
        ) = stored[l]
        g_low = gradient.astype(BF)
        g_all = gather_pair(g_low)
        grad_down_b = jnp.sum(g_low.astype(F32), axis=0)
        grad_activated = dot(g_all, w_back, ((1,), (0,)))
        grad_inner = (grad_activated * gelu_slope(inner)).astype(BF)
        grad_fc_b = jnp.sum(grad_inner.astype(F32), axis=0)
        hidden_sums[l] = to_owner(
            hidden_grads(
                normed_two_all, grad_inner, g_all, activated, head_grads if l == 0 else None
            ),
            1 - l,
        )
        grad_two = sum_pair(dot(grad_inner, w_up, ((1,), (1,))))
        dx, gain_two, shift_two = norm_backward(grad_two, xhat_two, rstd_two, gains[l, 1], mask)
        grad_middle = gradient + dx
        m_low = grad_middle.astype(BF)
        m_all = gather_rows(m_low)
        grad_out_b = jnp.sum(m_low.astype(F32), axis=0)
        grad_heads = project(m_all, w_heads, 3 * QW, HW, jnp.zeros((QW,), F32))
        grad_qkv = attend_backward(live, places, log_total, grad_heads, qkv)
        if l == 0:
            hidden_own = [None, own_hidden(hidden_sums[1])]
            grad_qkv, hidden_own[1] = lax.optimization_barrier((grad_qkv, hidden_own[1]))
        qkv_b = jnp.sum(grad_qkv.astype(F32), axis=0)
        grad_one, head_grads = sum_rows(
            grad_qkv,
            w_heads,
            0,
            3 * QW,
            lambda rows: head_grads_of(normed_all, rows, m_all, attended),
            apart=l == 0,
        )
        dx, gain_one, shift_one = norm_backward(grad_one, xhat, rstd, gains[l, 0], mask)
        gradient = grad_middle + dx
        small[l] = [gain_one, gain_two, shift_one, shift_two, grad_out_b, grad_down_b]
        fc_biases.append(
            jnp.where(high, jnp.roll(grad_fc_b, FR), grad_fc_b)
        )
        head_biases.append(qkv_b)

    head_sum_a = to_shards(head_grads)

    line = sum_line_parts(
        jnp.stack(small[0] + small[1]),
        jnp.pad(jnp.stack(fc_biases[::-1]), ((0, 0), (0, 2 * DP - FC))).reshape(4, DP),
    )
    own = jnp.pad(jnp.stack(head_biases[::-1]), ((0, 0), (0, DP - 3 * QW)))
    other = swap_ctx(own)
    both = jnp.concatenate([jnp.where(first, own, other), jnp.where(first, other, own)], axis=0)
    sums = sum_shards(jnp.concatenate([line, both], axis=0), 1)
    sums, head_sum_a, hidden_sums[0] = lax.optimization_barrier(
        (sums, head_sum_a, hidden_sums[0])
    )
    sums = sum_shards(sums, 4)
    head_sums = jnp.concatenate(
        [jnp.sum(head_sum_a.astype(F32), axis=0).astype(BF), hidden_sums[0][:, 2 * FC :]], axis=1
    )
    sums, head_sums = lax.optimization_barrier((sums, head_sums))
    vectors = narrow(sums[:12]).reshape(LAYERS, 6, D)
    fc_sum = sums[12:16].reshape(LAYERS, 2 * DP)
    fc_sum = jnp.where(high, fc_sum[:, FR : 2 * FR], fc_sum[:, :FR])
    halves = sums[16:].reshape(2, LAYERS, DP)[:, :, : 3 * QW].reshape(2, LAYERS, 3, 3, HD)
    head_sum = jnp.concatenate([halves[0], halves[1, :, :2]], axis=1)
    head_sum = jnp.concatenate([head_sum[:, :, 0], head_sum[:, :, 2]], axis=-1)

    def own_features(v):
        keep = jnp.where(first, v[:WIDE], v[WIDE:])
        recv = swap_ctx(jnp.where(first, v[WIDE:], v[:WIDE]))
        return (
            jnp.where(first, keep, recv)[:CHUNK].astype(F32),
            jnp.where(first, recv, keep)[:CHUNK].astype(F32),
        )

    halves = own_features(head_sums)
    hidden_own[0] = own_hidden(hidden_sums[0][:, : 2 * FC])
    grads = [[], [], [], []]
    for l in range(LAYERS):
        a, b = [v[:, l * HW : (l + 1) * HW] for v in halves]
        qkv = jnp.concatenate([a[:, : 3 * QW], b[:, : 2 * QW]], axis=1).reshape(CHUNK, 5, 3 * HD)
        grads[0].append(jnp.moveaxis(qkv, 1, 0))
        outs = jnp.concatenate([a[:, 3 * QW :], b[:, 3 * QW : 3 * QW + 2 * HD]], axis=1)
        grads[1].append(outs.T.reshape(5, HD, CHUNK))
        both = hidden_own[l]
        grads[2].append(both[:, :FR])
        grads[3].append(both[:, FR:].T)

    return (
        mixed[None],
        narrow(gradient)[None],
        vectors[:, 0:2],
        vectors[:, 2:4],
        jnp.stack(grads[0])[:, None],
        head_sum[:, None],
        jnp.stack(grads[1])[:, None],
        vectors[:, 4],
        jnp.stack(grads[2]),
        fc_sum,
        jnp.stack(grads[3]),
        vectors[:, 5],
    )


def solution(mesh):
    in_specs = (
        P("shard", ("ctx", "tp"), None),
        P("shard", ("ctx", "tp"), None),
        P(),
        P(),
        P(),
        P(),
        P(None, "tp", None, ("shard", "ctx"), None),
        P(None, "tp", None, None),
        P(None, "tp", None, None, ("shard", "ctx")),
        P(),
        P(None, ("shard", "ctx"), "tp"),
        P(None, "tp"),
        P(None, "tp", ("shard", "ctx")),
        P(),
    )
    out_specs = (
        P("shard", ("ctx", "tp"), None),
        P("shard", ("ctx", "tp"), None),
        P(),
        P(),
        P(None, "tp", None, ("shard", "ctx"), None),
        P(None, "tp", None, None),
        P(None, "tp", None, None, ("shard", "ctx")),
        P(),
        P(None, ("shard", "ctx"), "tp"),
        P(None, "tp"),
        P(None, "tp", ("shard", "ctx")),
        P(),
    )
    return jax.shard_map(shards, mesh=mesh, in_specs=in_specs, out_specs=out_specs, check_vma=False)
```

```python
import jax
import jax.numpy as jnp
from jax import lax
from jax.experimental import pallas as pl
from jax.experimental.pallas import tpu as pltpu
from jax.sharding import PartitionSpec as P

D = 1088
HD = 64
LAYERS = 2
EPS = 1e-05
SHARDS = 16
CHUNK = 34
WIDE = 36
DP = 2 * SHARDS * WIDE
HEADS_HERE = 3
QW = HEADS_HERE * HD
FR = 1088
FC = 2 * FR
HW = 4 * QW
ROWS = 128
BF = jnp.bfloat16
F32 = jnp.float32
LINE = ("ctx", "tp")


def line_perm(target):
    pairs = []
    for c in range(2):
        for h in range(2):
            for k in range(2):
                x2, k2 = target(2 * h + c, k)
                pairs.append((c * 4 + h * 2 + k, (x2 % 2) * 4 + (x2 // 2) * 2 + k2))
    return pairs


def swap_core(v):
    return lax.ppermute(v, LINE, line_perm(lambda x, k: (x, 1 - k)))


def swap_x(v, m):
    return lax.ppermute(v, LINE, line_perm(lambda x, k: (x ^ m, k)))


def swap_ctx(v):
    return lax.ppermute(v, "ctx", [(0, 1), (1, 0)])


def swap_shard(v, m):
    return lax.ppermute(v, "shard", [(i, i ^ m) for i in range(SHARDS)])


def gather_shards(copies):
    return lax.all_to_all(copies, "shard", 0, 0, tiled=True).reshape(-1, copies.shape[2])


def to_shards(v):
    v = v.reshape(SHARDS, v.shape[0] // SHARDS, v.shape[1])
    return lax.all_to_all(v, "shard", 0, 0, tiled=True)


def gather_pair(piece):
    return jnp.concatenate([piece, swap_core(piece)], axis=0)


def sum_pair(partial):
    return partial[:ROWS] + swap_core(partial[ROWS:].astype(BF)).astype(F32)


def gather_rows(piece):
    mine = jnp.concatenate([piece] + [swap_x(piece, m) for m in (1, 2, 3)], axis=0)
    return mine, swap_core(mine)


def sum_rows(rows, w, lo, hi, beside=None, apart=False):
    arrived = swap_core(dot(rows[HALF:], w[:, lo:hi], ((1,), (1,))).astype(BF))
    own, *others = chip_sum(rows, w, arrived, lo, hi)
    parts = [swap_x(v, m) for m, v in zip((1, 2, 3), others)]
    extra = None
    if beside is not None:
        own, rows = lax.optimization_barrier((own, rows))
        extra = beside(rows)
        if not apart:
            parts, extra = lax.optimization_barrier((parts, extra))
    parts = [v.astype(F32) for v in parts]
    return (own + parts[0]) + (parts[1] + parts[2]), extra


def sum_shards(v, step):
    return (v + swap_shard(v, step)) + (swap_shard(v, 2 * step) + swap_shard(v, 3 * step))


def sum_line_parts(both_cores, each_core):
    v = jnp.concatenate([both_cores + swap_core(both_cores), each_core], axis=0)
    return (v + swap_x(v, 1)) + (swap_x(v, 2) + swap_x(v, 3))


def dot(a, b, dims):
    return lax.dot_general(a, b, (dims, ((), ())), preferred_element_type=F32)


def norm_forward(x, gain, shift, mask):
    mean = jnp.sum(x, axis=-1, keepdims=True) * (1.0 / D)
    centred = (x - mean) * mask
    var = jnp.sum(centred * centred, axis=-1, keepdims=True) * (1.0 / D)
    rstd = lax.rsqrt(var + EPS)
    xhat = centred * rstd
    return (xhat * gain + shift).astype(BF), xhat, rstd


def norm_backward(dy, xhat, rstd, gain, mask):
    e = dy * gain
    mean_e = jnp.sum(e, axis=-1, keepdims=True) * (1.0 / D)
    mean_ex = jnp.sum(e * xhat, axis=-1, keepdims=True) * (1.0 / D)
    dx = rstd * (e - mean_e - xhat * mean_ex) * mask
    return dx, jnp.sum(dy * xhat, axis=0), jnp.sum(dy, axis=0)


def normal_cdf(v):
    return 0.5 + 0.5 * lax.erf(v * 0.5**0.5)


def gelu_slope(v):
    return normal_cdf(v) + v * jnp.exp(-0.5 * v * v) * (2 * jnp.pi) ** -0.5


LINE_ROWS = 8 * ROWS
Q_ROWS = 256
PLAIN = (((1,), (0,)), ((), ()))
TURN_RIGHT = (((1,), (1,)), ((), ()))
TURN_LEFT = (((0,), (0,)), ((), ()))


def mul(a, b, dims):
    return lax.dot_general(a, b, dims, preferred_element_type=F32)


def head_parts(ref, rows, j):
    at = 3 * HD * j
    return [ref[rows, at + i * HD : at + (i + 1) * HD] for i in range(3)]


def attend_body(live_ref, kp_ref, qp_ref, qkv_ref, out_ref, lse_ref):
    mine = pl.ds(pl.multiple_of(pl.program_id(0) * Q_ROWS, Q_ROWS), Q_ROWS)
    allowed = kp_ref[...] <= qp_ref[...]
    for j in range(HEADS_HERE):
        queries = qkv_ref[mine, 3 * HD * j : 3 * HD * j + HD]
        _, keys, values = head_parts(qkv_ref, slice(None), j)
        scores = jnp.where(allowed, mul(keys, queries, TURN_RIGHT) * HD**-0.5, -1e30)
        highest = jnp.max(scores, axis=0, keepdims=True)
        exponent = jnp.exp(scores - highest)
        totals = jnp.sum(exponent, axis=0, keepdims=True)
        probs = (exponent * (1.0 / totals)).astype(BF)
        heads = mul(values, probs, TURN_LEFT) * live_ref[j]
        out_ref[:, j * HD : (j + 1) * HD] = heads.T.astype(BF)
        lse_ref[j : j + 1, :] = highest + jnp.log(totals)
    lse_ref[HEADS_HERE:, :] = jnp.zeros((8 - HEADS_HERE, Q_ROWS), F32)


def attend_back_body(
    live_ref, kp_ref, qp_ref, lse_ref, dout_ref, qkv_ref, out_ref, key_sum, value_sum
):
    step = pl.program_id(0)
    mine = pl.ds(pl.multiple_of(step * Q_ROWS, Q_ROWS), Q_ROWS)
    allowed = kp_ref[...] <= qp_ref[...]

    @pl.when(step == 0)
    def _():
        key_sum[...] = jnp.zeros_like(key_sum)
        value_sum[...] = jnp.zeros_like(value_sum)

    for j in range(HEADS_HERE):
        queries = qkv_ref[mine, 3 * HD * j : 3 * HD * j + HD]
        _, keys, values = head_parts(qkv_ref, slice(None), j)
        dout = dout_ref[:, j * HD : (j + 1) * HD] * live_ref[j].astype(BF)
        scores = jnp.where(allowed, mul(keys, queries, TURN_RIGHT) * HD**-0.5, -1e30)
        probs = jnp.exp(scores - lse_ref[j : j + 1, :])
        dprobs = mul(values, dout, TURN_RIGHT)
        dscores = probs * (dprobs - jnp.sum(dprobs * probs, axis=0, keepdims=True))
        dscores = dscores.astype(BF)
        value_sum[j] += mul(probs.astype(BF), dout, PLAIN)
        key_sum[j] += mul(dscores, queries, PLAIN)
        dqueries = mul(keys, dscores, TURN_LEFT) * HD**-0.5
        out_ref[mine, 3 * HD * j : 3 * HD * j + HD] = dqueries.T.astype(BF)

    @pl.when(step == LINE_ROWS // Q_ROWS - 1)
    def _():
        for j in range(HEADS_HERE):
            at = 3 * HD * j
            out_ref[:, at + HD : at + 2 * HD] = (key_sum[j] * HD**-0.5).astype(BF)
            out_ref[:, at + 2 * HD : at + 3 * HD] = value_sum[j].astype(BF)


def attend_specs():
    return [
        pl.BlockSpec(memory_space=pltpu.SMEM),
        pl.BlockSpec((LINE_ROWS, 1), lambda i: (0, 0)),
        pl.BlockSpec((1, Q_ROWS), lambda i: (0, i)),
    ]


def attend_forward(live, places, qkv):
    return pl.pallas_call(
        attend_body,
        grid=(LINE_ROWS // Q_ROWS,),
        in_specs=attend_specs() + [pl.BlockSpec((LINE_ROWS, 3 * QW), lambda i: (0, 0))],
        out_specs=[
            pl.BlockSpec((Q_ROWS, QW), lambda i: (i, 0)),
            pl.BlockSpec((8, Q_ROWS), lambda i: (0, i)),
        ],
        out_shape=[
            jax.ShapeDtypeStruct((LINE_ROWS, QW), BF),
            jax.ShapeDtypeStruct((8, LINE_ROWS), F32),
        ],
        compiler_params=pltpu.CompilerParams(vmem_limit_bytes=48 << 20),
        cost_estimate=pl.CostEstimate(
            flops=4 * HEADS_HERE * LINE_ROWS * LINE_ROWS * HD * 4,
            bytes_accessed=LINE_ROWS * 4 * QW * 2,
            transcendentals=HEADS_HERE * LINE_ROWS * LINE_ROWS,
        ),
        name="attend",
    )(live, places[:, None], places[None, :], qkv)


def attend_backward(live, places, lse, dout, qkv):
    return pl.pallas_call(
        attend_back_body,
        grid=(LINE_ROWS // Q_ROWS,),
        in_specs=attend_specs()
        + [
            pl.BlockSpec((8, Q_ROWS), lambda i: (0, i)),
            pl.BlockSpec((Q_ROWS, QW), lambda i: (i, 0)),
            pl.BlockSpec((LINE_ROWS, 3 * QW), lambda i: (0, 0)),
        ],
        out_specs=pl.BlockSpec((LINE_ROWS, 3 * QW), lambda i: (0, 0)),
        out_shape=jax.ShapeDtypeStruct((LINE_ROWS, 3 * QW), BF),
        scratch_shapes=[pltpu.VMEM((HEADS_HERE, LINE_ROWS, HD), F32)] * 2,
        compiler_params=pltpu.CompilerParams(vmem_limit_bytes=48 << 20),
        cost_estimate=pl.CostEstimate(
            flops=10 * HEADS_HERE * LINE_ROWS * LINE_ROWS * HD * 4,
            bytes_accessed=LINE_ROWS * 7 * QW * 2,
            transcendentals=HEADS_HERE * LINE_ROWS * LINE_ROWS,
        ),
        name="attend_back",
    )(live, places[:, None], places[None, :], lse, dout, qkv)


def head_halves(w_qkv, w_out):
    cols = jnp.moveaxis(w_qkv, 0, 1).reshape(CHUNK, 15 * HD)
    outs = w_out.reshape(5 * HD, CHUNK).T
    gap = ((0, 0), (0, HD))
    return (
        jnp.concatenate([cols[:, : 3 * QW], outs[:, :QW]], axis=1),
        jnp.concatenate(
            [jnp.pad(cols[:, 3 * QW :], ((0, 0), (0, QW))), jnp.pad(outs[:, QW:], gap)], axis=1
        ),
    )


HALF = 4 * ROWS
GRAD_ROWS = 384


def project(pair, w, lo, hi, bias):
    def body(mine, other, w_ref, bias_ref, out_ref):
        for at, x in ((0, mine), (HALF, other)):
            got = mul(x[...], w_ref[:, lo:hi], PLAIN) + bias_ref[...]
            out_ref[at : at + HALF, :] = got.astype(BF)

    half = pl.BlockSpec((HALF, DP), lambda i: (0, 0))
    return pl.pallas_call(
        body,
        grid=(1,),
        in_specs=[
            half,
            half,
            pl.BlockSpec((DP, HW), lambda i: (0, 0)),
            pl.BlockSpec((1, hi - lo), lambda i: (0, 0)),
        ],
        out_specs=pl.BlockSpec((2 * HALF, hi - lo), lambda i: (0, 0)),
        out_shape=jax.ShapeDtypeStruct((2 * HALF, hi - lo), BF),
        compiler_params=pltpu.CompilerParams(vmem_limit_bytes=48 << 20),
        cost_estimate=pl.CostEstimate(
            flops=4 * HALF * DP * (hi - lo), bytes_accessed=8 << 20, transcendentals=0
        ),
        name="project",
    )(*pair, w, bias.reshape(1, hi - lo))


def chip_sum(rows, w, arrived, lo, hi):
    def body(rows_ref, w_ref, arrived_ref, *outs):
        w_part = w_ref[:, lo:hi]
        for m, out in enumerate(outs):
            block = slice(m * ROWS, (m + 1) * ROWS)
            got = mul(rows_ref[block, :], w_part, TURN_RIGHT) + arrived_ref[block, :].astype(F32)
            out[...] = got.astype(out.dtype)

    return pl.pallas_call(
        body,
        grid=(1,),
        in_specs=[
            pl.BlockSpec((HALF, hi - lo), lambda i: (0, 0)),
            pl.BlockSpec((DP, HW), lambda i: (0, 0)),
            pl.BlockSpec((HALF, DP), lambda i: (0, 0)),
        ],
        out_specs=[pl.BlockSpec((ROWS, DP), lambda i: (0, 0))] * 4,
        out_shape=[jax.ShapeDtypeStruct((ROWS, DP), F32 if m == 0 else BF) for m in range(4)],
        compiler_params=pltpu.CompilerParams(vmem_limit_bytes=48 << 20),
        cost_estimate=pl.CostEstimate(
            flops=2 * HALF * DP * (hi - lo), bytes_accessed=6 << 20, transcendentals=0
        ),
        name="chip_sum",
    )(rows, w, arrived)


def head_grads_of(pair, dqkv, m_pair, attended):
    def body(x0, x1, m0, m1, dqkv_ref, att_ref, out_ref):
        got = mul(x0[...], dqkv_ref[:HALF, :], TURN_LEFT)
        got += mul(x1[...], dqkv_ref[HALF:, :], TURN_LEFT)
        out_ref[:, : 3 * QW] = got.astype(BF)
        got = mul(m0[...], att_ref[:HALF, :], TURN_LEFT)
        got += mul(m1[...], att_ref[HALF:, :], TURN_LEFT)
        out_ref[:, 3 * QW :] = got.astype(BF)

    feature = pl.BlockSpec((HALF, GRAD_ROWS), lambda i: (0, i))
    return pl.pallas_call(
        body,
        grid=(DP // GRAD_ROWS,),
        in_specs=[feature] * 4
        + [
            pl.BlockSpec((2 * HALF, 3 * QW), lambda i: (0, 0)),
            pl.BlockSpec((2 * HALF, QW), lambda i: (0, 0)),
        ],
        out_specs=pl.BlockSpec((GRAD_ROWS, HW), lambda i: (i, 0)),
        out_shape=jax.ShapeDtypeStruct((DP, HW), BF),
        compiler_params=pltpu.CompilerParams(vmem_limit_bytes=48 << 20),
        cost_estimate=pl.CostEstimate(
            flops=4 * HALF * DP * HW, bytes_accessed=8 << 20, transcendentals=0
        ),
        name="head_grads",
    )(*pair, *m_pair, dqkv, attended)


def hidden_grads_body(heads, x_ref, dinner_ref, g_ref, act_ref, *refs):
    out_ref = refs[-1]
    turned = (((0,), (0,)), ((), ()))
    out_ref[:, :FC] = lax.dot_general(
        x_ref[...], dinner_ref[...], turned, preferred_element_type=F32
    ).astype(BF)
    out_ref[:, FC : 2 * FC] = lax.dot_general(
        g_ref[...], act_ref[...], turned, preferred_element_type=F32
    ).astype(BF)
    if heads:
        out_ref[:, 2 * FC :] = refs[0][...]


def hidden_grads(x, dinner, g, act, head_grads=None):
    rows = x.shape[0]
    wide = 2 * FC + (0 if head_grads is None else HW)
    args = [x, dinner, g, act] + ([] if head_grads is None else [head_grads])
    feature = pl.BlockSpec((rows, GRAD_ROWS), lambda i: (0, i))
    whole = pl.BlockSpec((rows, FC), lambda i: (0, 0))
    specs = [feature, whole, feature, whole]
    if head_grads is not None:
        specs.append(pl.BlockSpec((GRAD_ROWS, HW), lambda i: (i, 0)))
    return pl.pallas_call(
        lambda *refs: hidden_grads_body(head_grads is not None, *refs),
        grid=(DP // GRAD_ROWS,),
        in_specs=specs,
        out_specs=pl.BlockSpec((GRAD_ROWS, wide), lambda i: (i, 0)),
        out_shape=jax.ShapeDtypeStruct((DP, wide), BF),
        compiler_params=pltpu.CompilerParams(vmem_limit_bytes=48 << 20),
        cost_estimate=pl.CostEstimate(
            flops=4 * rows * DP * FC, bytes_accessed=2 * DP * wide, transcendentals=0
        ),
        name="hidden_grads",
    )(*args)


def shards(
    tokens,
    cotangent,
    block_order,
    head_count,
    ln_gain,
    ln_bias,
    w_qkv,
    b_qv,
    w_out,
    b_out,
    w_fc,
    b_fc,
    w_down,
    b_down,
):
    ctx = lax.axis_index("ctx")
    tp = lax.axis_index("tp")
    first = ctx == 0

    wide = jnp.arange(DP, dtype=jnp.int32)
    inside = wide % WIDE
    source = jnp.where(inside < CHUNK, wide // WIDE * CHUNK + inside, -1)
    spread = (source[None, :] == jnp.arange(D, dtype=jnp.int32)[:, None]).astype(BF)
    mask = (inside < CHUNK).astype(F32)[None, :]

    def widen(v):
        full = v.reshape(-1, D)
        out = lax.dot_general(
            full,
            spread.astype(full.dtype),
            (((1,), (0,)), ((), ())),
            precision=lax.Precision.HIGHEST if full.dtype == F32 else None,
            preferred_element_type=F32,
        )
        return out.reshape(*v.shape[:-1], DP)

    def narrow(v):
        return lax.dot_general(
            v,
            spread.astype(v.dtype),
            (((1,), (1,)), ((), ())),
            precision=lax.Precision.HIGHEST if v.dtype == F32 else None,
            preferred_element_type=F32,
        )

    def exchanged(halves):
        keep = jnp.where(first, halves[0], halves[1])
        send = jnp.where(first, halves[1], halves[0])
        recv = swap_ctx(send)
        top = jnp.where(first, keep, recv)
        low = jnp.where(first, recv, keep)
        gap = ((0, WIDE - CHUNK), (0, 0))
        return jnp.concatenate([jnp.pad(top, gap), jnp.pad(low, gap)], axis=0)

    def exchanged_hidden(w_fc, w_down):
        raw = jnp.concatenate([w_fc, w_down], axis=1)
        raw = jnp.pad(raw, ((0, WIDE - CHUNK), (0, 0)))
        p = [raw] + [swap_x(raw, m) for m in (1, 2, 3)]
        own, other = [
            jnp.concatenate([jnp.where(first, a, b), jnp.where(first, b, a)], axis=0)
            for a, b in ((p[0], p[1]), (p[2], p[3]))
        ]
        return jnp.concatenate([own[:, :FR], other[:, :FR], own[:, FR:], other[:, FR:]], axis=1)

    def fetch(pack):
        return lax.all_gather(pack, "shard", axis=0, tiled=True)

    hidden_a = exchanged_hidden(w_fc[0], w_down[0].T)
    heads_b = exchanged(head_halves(w_qkv[1, 0], w_out[1, 0]))
    joined, w_qkv_a, w_out_a = lax.optimization_barrier(
        (jnp.concatenate([heads_b, hidden_a], axis=1), w_qkv[0, 0], w_out[0, 0])
    )
    fetched_a = fetch(joined)
    pack_a = exchanged(head_halves(w_qkv_a, w_out_a))
    copies = jnp.broadcast_to(pack_a, (SHARDS, *pack_a.shape))
    weights = [
        (None, fetched_a[:, HW : HW + FC], fetched_a[:, HW + FC :]),
        (fetched_a, None, None),
    ]

    core = tp % 2
    x = (tp // 2) * 2 + ctx
    units = []
    for j in range(2):
        for m in range(4):
            chip = x ^ m
            block = (chip % 2) * 2 + chip // 2
            start = jnp.sum(jnp.where(jnp.arange(4) == block, block_order, 0)) * 256
            units.append(start + (core ^ j) * ROWS + jnp.arange(ROWS, dtype=jnp.int32))
    places = jnp.concatenate(units)
    my_count = jnp.sum(jnp.where(jnp.arange(4) == tp, head_count, 0))
    slot = jnp.arange(HEADS_HERE, dtype=jnp.int32) + ctx * HEADS_HERE
    live = ((slot < my_count) & (slot < 5)).astype(F32)

    head_bias = jnp.pad(b_qv[:, 0], ((0, 0), (0, 1), (0, 0)))
    head_bias = jnp.where(first, head_bias[:, :3], head_bias[:, 3:])
    head_bias = jnp.concatenate(
        [head_bias[..., :HD], jnp.zeros_like(head_bias[..., :HD]), head_bias[..., HD:]], axis=-1
    ).reshape(LAYERS, 3 * QW)
    fc_bias = jnp.concatenate([b_fc, swap_x(b_fc, 2)], axis=1)

    vectors = widen(
        jnp.concatenate([ln_gain.reshape(4, D), ln_bias.reshape(4, D), b_out, b_down], axis=0)
    )
    gains = vectors[0:4].reshape(LAYERS, 2, DP)
    shifts = vectors[4:8].reshape(LAYERS, 2, DP)
    out_bias, down_bias = vectors[8:10], vectors[10:12]

    hidden = widen(tokens[0])
    gradient = widen(cotangent[0])
    stored = []
    for l in range(LAYERS):
        w_heads = weights[l][0]
        normed, xhat, rstd = norm_forward(hidden, gains[l, 0], shifts[l, 0], mask)
        if l == 0:
            normed, copies = lax.optimization_barrier((normed, copies))
            w_heads, w_fc_b, w_down_b = lax.optimization_barrier(
                (gather_shards(copies), w_fc[1], w_down[1].T)
            )
            hidden_b = exchanged_hidden(w_fc_b, w_down_b)
            weights[0] = (w_heads, *weights[0][1:])
        normed_all = gather_rows(normed)
        qkv = project(normed_all, w_heads, 0, 3 * QW, head_bias[l])
        attended, log_total = attend_forward(live, places, qkv)
        if l == 0:
            attended, hidden_b = lax.optimization_barrier((attended, hidden_b))
            fetched_b = fetch(hidden_b)
            weights[1] = (fetched_a, fetched_b[:, :FC], fetched_b[:, FC:])
        summed, _ = sum_rows(attended, w_heads, 3 * QW, HW)
        middle = hidden + (summed + out_bias[l])
        normed_two, xhat_two, rstd_two = norm_forward(middle, gains[l, 1], shifts[l, 1], mask)
        normed_two_all = gather_pair(normed_two)
        _, w_up, w_back = weights[l]
        inner = dot(normed_two_all, w_up, ((1,), (0,))) + fc_bias[l]
        activated = (inner * normal_cdf(inner)).astype(BF)
        down_out = dot(activated, w_back, ((1,), (1,)))
        hidden = middle + (sum_pair(down_out) + down_bias[l])
        stored.append(
            (
                normed_all,
                xhat,
                rstd,
                qkv,
                log_total,
                attended,
                normed_two_all,
                xhat_two,
                rstd_two,
                inner,
                activated,
            )
        )
    mixed = narrow(hidden.astype(BF)).astype(BF)

    small = [None] * LAYERS
    fc_biases, head_biases = [], []
    high = tp // 2 == 1
    hidden_sums = [None] * LAYERS

    def own_hidden(v):
        mine = jnp.where(first, v[:WIDE], v[WIDE:])
        theirs = jnp.where(first, v[WIDE:], v[:WIDE])

        def piece(rows, h):
            return jnp.concatenate(
                [rows[:, h * FR : (h + 1) * FR], rows[:, FC + h * FR : FC + (h + 1) * FR]], axis=1
            )

        came = [swap_x(piece(theirs if m % 2 else mine, m // 2), m).astype(F32) for m in (1, 2, 3)]
        both = ((piece(mine, 0).astype(F32) + came[0]) + (came[1] + came[2]))[:CHUNK]
        return both[:, :FR], both[:, FR:].T

    def to_owner(v, dim):
        v = v.reshape((1,) * dim + v.shape)
        v = lax.psum_scatter(v, "shard", scatter_dimension=dim, tiled=True)
        return lax.optimization_barrier(v).reshape(v.shape[-2:])

    for l in reversed(range(LAYERS)):
        w_heads, w_up, w_back = weights[l]
        (
            normed_all,
            xhat,
            rstd,
            qkv,
            log_total,
            attended,
            normed_two_all,
            xhat_two,
            rstd_two,
            inner,
            activated,
        ) = stored[l]
        g_low = gradient.astype(BF)
        g_all = gather_pair(g_low)
        grad_down_b = jnp.sum(g_low.astype(F32), axis=0)
        grad_activated = dot(g_all, w_back, ((1,), (0,)))
        grad_inner = (grad_activated * gelu_slope(inner)).astype(BF)
        grad_fc_b = jnp.sum(grad_inner.astype(F32), axis=0)
        hidden_sums[l] = to_owner(
            hidden_grads(
                normed_two_all, grad_inner, g_all, activated, head_grads if l == 0 else None
            ),
            1 - l,
        )
        grad_two = sum_pair(dot(grad_inner, w_up, ((1,), (1,))))
        dx, gain_two, shift_two = norm_backward(grad_two, xhat_two, rstd_two, gains[l, 1], mask)
        grad_middle = gradient + dx
        m_low = grad_middle.astype(BF)
        m_all = gather_rows(m_low)
        grad_out_b = jnp.sum(m_low.astype(F32), axis=0)
        grad_heads = project(m_all, w_heads, 3 * QW, HW, jnp.zeros((QW,), F32))
        grad_qkv = attend_backward(live, places, log_total, grad_heads, qkv)
        if l == 0:
            hidden_own = [None, own_hidden(hidden_sums[1])]
            grad_qkv, hidden_own[1] = lax.optimization_barrier((grad_qkv, hidden_own[1]))
        qkv_b = jnp.sum(grad_qkv.astype(F32), axis=0)
        grad_one, head_grads = sum_rows(
            grad_qkv,
            w_heads,
            0,
            3 * QW,
            lambda rows: head_grads_of(normed_all, rows, m_all, attended),
            apart=l == 0,
        )
        dx, gain_one, shift_one = norm_backward(grad_one, xhat, rstd, gains[l, 0], mask)
        gradient = grad_middle + dx
        small[l] = [gain_one, gain_two, shift_one, shift_two, grad_out_b, grad_down_b]
        fc_biases.append(
            jnp.where(high, jnp.roll(grad_fc_b, FR), grad_fc_b)
        )
        head_biases.append(qkv_b)

    head_sum_a = to_shards(head_grads)

    line = sum_line_parts(
        jnp.stack(small[0] + small[1]),
        jnp.pad(jnp.stack(fc_biases[::-1]), ((0, 0), (0, 2 * DP - FC))).reshape(4, DP),
    )
    own = jnp.pad(jnp.stack(head_biases[::-1]), ((0, 0), (0, DP - 3 * QW)))
    other = swap_ctx(own)
    both = jnp.concatenate([jnp.where(first, own, other), jnp.where(first, other, own)], axis=0)
    sums = sum_shards(jnp.concatenate([line, both], axis=0), 1)
    sums, head_sum_a, hidden_sums[0] = lax.optimization_barrier(
        (sums, head_sum_a, hidden_sums[0])
    )
    sums = sum_shards(sums, 4)
    head_sums = jnp.concatenate(
        [jnp.sum(head_sum_a.astype(F32), axis=0).astype(BF), hidden_sums[0][:, 2 * FC :]], axis=1
    )
    sums, head_sums = lax.optimization_barrier((sums, head_sums))
    vectors = narrow(sums[:12]).reshape(LAYERS, 6, D)
    fc_sum = sums[12:16].reshape(LAYERS, 2 * DP)
    fc_sum = jnp.where(high, fc_sum[:, FR : 2 * FR], fc_sum[:, :FR])
    halves = sums[16:].reshape(2, LAYERS, DP)[:, :, : 3 * QW].reshape(2, LAYERS, 3, 3, HD)
    head_sum = jnp.concatenate([halves[0], halves[1, :, :2]], axis=1)
    head_sum = jnp.concatenate([head_sum[:, :, 0], head_sum[:, :, 2]], axis=-1)

    def own_features(v):
        keep = jnp.where(first, v[:WIDE], v[WIDE:])
        recv = swap_ctx(jnp.where(first, v[WIDE:], v[:WIDE]))
        return (
            jnp.where(first, keep, recv)[:CHUNK].astype(F32),
            jnp.where(first, recv, keep)[:CHUNK].astype(F32),
        )

    halves = own_features(head_sums)
    hidden_own[0] = own_hidden(hidden_sums[0][:, : 2 * FC])
    grads = [[], [], [], []]
    for l in range(LAYERS):
        a, b = [v[:, l * HW : (l + 1) * HW] for v in halves]
        qkv = jnp.concatenate([a[:, : 3 * QW], b[:, : 2 * QW]], axis=1).reshape(CHUNK, 5, 3 * HD)
        grads[0].append(jnp.moveaxis(qkv, 1, 0))
        outs = jnp.concatenate([a[:, 3 * QW :], b[:, 3 * QW : 3 * QW + 2 * HD]], axis=1)
        grads[1].append(outs.T.reshape(5, HD, CHUNK))
        grads[2].append(hidden_own[l][0])
        grads[3].append(hidden_own[l][1])

    return (
        mixed[None],
        narrow(gradient)[None],
        vectors[:, 0:2],
        vectors[:, 2:4],
        jnp.stack(grads[0])[:, None],
        head_sum[:, None],
        jnp.stack(grads[1])[:, None],
        vectors[:, 4],
        jnp.stack(grads[2]),
        fc_sum,
        jnp.stack(grads[3]),
        vectors[:, 5],
    )


def solution(mesh):
    in_specs = (
        P("shard", ("ctx", "tp"), None),
        P("shard", ("ctx", "tp"), None),
        P(),
        P(),
        P(),
        P(),
        P(None, "tp", None, ("shard", "ctx"), None),
        P(None, "tp", None, None),
        P(None, "tp", None, None, ("shard", "ctx")),
        P(),
        P(None, ("shard", "ctx"), "tp"),
        P(None, "tp"),
        P(None, "tp", ("shard", "ctx")),
        P(),
    )
    out_specs = (
        P("shard", ("ctx", "tp"), None),
        P("shard", ("ctx", "tp"), None),
        P(),
        P(),
        P(None, "tp", None, ("shard", "ctx"), None),
        P(None, "tp", None, None),
        P(None, "tp", None, None, ("shard", "ctx")),
        P(),
        P(None, ("shard", "ctx"), "tp"),
        P(None, "tp"),
        P(None, "tp", ("shard", "ctx")),
        P(),
    )
    return jax.shard_map(shards, mesh=mesh, in_specs=in_specs, out_specs=out_specs, check_vma=False)
```
